128 devices in a mesh: grp: 8 (over y, core), tile: 16 (over z, x).
Axes of the slice: x: 4, y: 4, z: 4, core: 2. Of those that a mesh axis runs over, the one named last changes fastest.
Arguments:
- prior_replicas: float32 [256, 8, 128, 1024], P('grp', None, 'tile'), may hold values from -140 to 140
- conductivity_map: float32 [8, 128, 1024], P(None, 'tile'), may hold values from 0.03 to 0.16
- member_slot: int32 [256], P('grp'), may hold values from 0 to 15, as said below
- merge_sketch: float32 [3, 32, 16], replicated, may hold values from -1 to 1
- obs_cells: int32 [4096], replicated, may hold values from 0 to 131071
- obs_values: float32 [4096], replicated, may hold values from -6 to 6
- obs_var: float32 [4096], replicated, may hold values from 30 to 300
Outputs:
- predicted_replicas: float32 [256, 8, 128, 1024], P('grp', None, 'tile')
- posterior_mean: float32 [128, 1024], P('tile', 'grp')
The draws below stay inside these ranges and needn't reach their ends.
Inputs may be any that keep to these rules, and one draw needn't show every extreme that they name: `member_slot`: within each group of 32 members every column 0 to 15 is named by exactly 2 members.
All inputs are finite; a program needn't handle non-finite values.
Results may differ from the reference program's by a relative error of at most 0.0001.
Values sent between devices are 32-bit elements; how exact they have to be, the bound alone decides.
No kernel may reach another device: no remote copies, remote signals or barrier semaphores. Data moves between devices by JAX's collectives and lax.ppermute only.
A program may use at most 128 MiB of HBM per device.

```python
import math
import jax
import jax.numpy as jnp
from jax import lax

DEPTH_TIERS = 8
GRID_SPAN_TWO = 1024
GROUP_MEMBERS = 32
BASIS_RANK = 16
NOBS = 4096
MERGES = 3
GRID_SPAN_ONE = 128
REPLICA_COUNT = 256
N_GRP = 8


def draw_prior_replicas(key, part):
    key = jax.random.fold_in(key, 11)
    first, second = jax.random.split(key, 2)
    shape = (REPLICA_COUNT, DEPTH_TIERS, GRID_SPAN_ONE, GRID_SPAN_TWO)
    member_scale = jnp.exp(jax.random.uniform(first, (REPLICA_COUNT, 1, 1, 1), jnp.float32, math.log(0.3), math.log(3.0)))
    along = 3.0 ** (jnp.arange(GRID_SPAN_ONE, dtype=jnp.float32) / max(GRID_SPAN_ONE - 1, 1))
    along = along.reshape(1, 1, GRID_SPAN_ONE, 1)
    noise = jnp.clip(jax.random.normal(second, shape, jnp.float32), -4.0, 4.0)
    value = noise * member_scale * along
    return value.astype(jnp.float32)


def draw_member_slot(key, part):
    key = jax.random.fold_in(key, 23)
    keys = jax.random.split(key, REPLICA_COUNT // GROUP_MEMBERS)
    orders = jax.vmap(lambda single: jax.random.permutation(single, GROUP_MEMBERS))(keys)
    return (orders % BASIS_RANK).reshape(-1).astype(jnp.int32)


def plant(array, stream_key, smallest, top_value):
    extent = array.shape
    spot = [jax.random.randint(jax.random.fold_in(stream_key, axis), (), 0, extent[axis]) for axis in range(len(extent))]
    array = array.at[tuple(spot)].set(smallest)
    longest = extent.index(max(extent))
    spot[longest] = (spot[longest] + 1) % extent[longest]
    return array.at[tuple(spot)].set(top_value)


def block_levels(key, extent, shards, low, largest):
    def one(axis_at, blocks):
        steps = jax.random.uniform(jax.random.fold_in(jax.random.fold_in(key, 6), axis_at), (blocks,), jnp.float32, low / len(shards), largest / len(shards))
        return jnp.repeat(jnp.exp(steps), extent[axis_at] // blocks).reshape((-1,) + (1,) * (len(extent) - axis_at - 1))

    factor_of = one(*shards[0])
    for cut in shards[1:]:
        factor_of = factor_of * one(*cut)
    return factor_of


def centred(rng, dims, scale, bound, kind=jnp.bfloat16):
    array = scale * jax.random.normal(rng, dims, jnp.float32)
    return jnp.clip(array, min=-bound, max=bound).astype(kind)


def setup_inputs(seed: int = 0) -> dict:
    splits = jax.random.split(jax.random.key(seed), 8)
    return {
        "prior_replicas": draw_prior_replicas(jax.random.fold_in(splits[7], 71), 0),
        "conductivity_map": jnp.clip(jnp.exp(math.log(0.16) - 1.6739764 * jax.random.uniform(splits[1], (DEPTH_TIERS, GRID_SPAN_ONE, GRID_SPAN_TWO), jnp.float32) ** block_levels(splits[1], (DEPTH_TIERS, GRID_SPAN_ONE, GRID_SPAN_TWO), ((1, 16),), -0.2, 0.2)), 0.03, 0.16),
        "member_slot": draw_member_slot(jax.random.fold_in(splits[7], 71), 0),
        "merge_sketch": centred(splits[3], (MERGES, 2 * BASIS_RANK, BASIS_RANK), (2 * BASIS_RANK) ** -0.5, 1.0, jnp.float32),
        "obs_cells": plant(jax.random.randint(splits[4], (NOBS,), 0, GRID_SPAN_ONE * GRID_SPAN_TWO), jax.random.fold_in(splits[4], 1), 0, (GRID_SPAN_ONE * GRID_SPAN_TWO) - 1).astype(jnp.int32),
        "obs_values": centred(splits[5], (NOBS,), 1.0, 6.0, jnp.float32),
        "obs_var": jnp.clip(jnp.exp(jax.random.uniform(splits[6], (NOBS,), jnp.float32, math.log(30.0), math.log(300.0))), 30.0, 300.0),
    }


def advance_timestep(heat_distribution, diffusivity):
    margined_grid = jnp.pad(heat_distribution, 1)
    lateral_neighbour = margined_grid[1:-1, 2:, 1:-1] + margined_grid[1:-1, :-2, 1:-1]
    lateral_neighbour = lateral_neighbour + margined_grid[1:-1, 1:-1, 2:] + margined_grid[1:-1, 1:-1, :-2]
    lateral_neighbour = lateral_neighbour + margined_grid[2:, 1:-1, 1:-1] + margined_grid[:-2, 1:-1, 1:-1]
    return heat_distribution + diffusivity * (lateral_neighbour - 6.0 * heat_distribution)

def compress(stack):
    grams = jnp.einsum('krc,ksc->krs', stack, stack, precision=lax.Precision.HIGHEST)
    lower = jnp.linalg.cholesky(grams)
    solved = jax.vmap(lambda a, b: jax.scipy.linalg.solve_triangular(a, b, lower=True))(lower, stack)
    scale = jnp.diagonal(lower, axis1=1, axis2=2)
    return solved * scale[:, :, None]

def reference(prior_replicas, conductivity_map, member_slot, merge_sketch, obs_cells, obs_values, obs_var):
    predicted_replicas = lax.map(lambda heat_distribution: advance_timestep(advance_timestep(heat_distribution, conductivity_map), conductivity_map), prior_replicas)
    uppermost_tier = predicted_replicas[:, DEPTH_TIERS - 1].reshape(REPLICA_COUNT, GRID_SPAN_ONE * GRID_SPAN_TWO)
    surface_mean = jnp.sum(uppermost_tier, axis=0) / REPLICA_COUNT
    member_deviations = uppermost_tier - surface_mean[None, :]
    indicator_vector = (member_slot[:, None] == jnp.arange(BASIS_RANK, dtype=jnp.int32)[None, :]).astype(jnp.float32)
    sketch_list = jnp.einsum('hxz,hxp->hzp', indicator_vector.reshape(N_GRP, GROUP_MEMBERS, BASIS_RANK), member_deviations.reshape(N_GRP, GROUP_MEMBERS, GRID_SPAN_ONE * GRID_SPAN_TWO), precision=lax.Precision.HIGHEST)
    stack = compress(sketch_list)
    for level in range(MERGES):
        joined = jnp.concatenate([stack[0::2], stack[1::2]], axis=1)
        mixed = jnp.einsum('kr,jkc->jrc', merge_sketch[level], joined, precision=lax.Precision.HIGHEST)
        stack = compress(mixed)
    basis = stack[0]
    picked = basis[:, obs_cells]
    innovation = obs_values - surface_mean[obs_cells]
    weighted = picked / obs_var[None, :]
    system = (REPLICA_COUNT - 1) * jnp.eye(BASIS_RANK, dtype=jnp.float32) + jnp.dot(weighted, picked.T, precision=lax.Precision.HIGHEST)
    rhs = jnp.dot(weighted, innovation, precision=lax.Precision.HIGHEST)
    factor = jnp.linalg.cholesky(system)
    coefficients = jax.scipy.linalg.cho_solve((factor, True), rhs)
    posterior_mean = surface_mean + jnp.dot(coefficients, basis, precision=lax.Precision.HIGHEST)
    return (predicted_replicas, posterior_mean.reshape(GRID_SPAN_ONE, GRID_SPAN_TWO))
```

```python
import jax
import jax.numpy as jnp
from jax import lax
from jax.experimental import pallas as pl
from jax.experimental.pallas import tpu as pltpu
from jax.sharding import PartitionSpec as P

HI = lax.Precision.HIGHEST
VMEM = pl.BlockSpec(memory_space=pltpu.VMEM)
SMEM = pl.BlockSpec(memory_space=pltpu.SMEM)
CHUNKS = (8, 8, 8, 8)
F32 = jnp.float32


def shape(*dims):
    return jax.ShapeDtypeStruct(dims, F32)


def cost(nbytes, flops=0):
    return pl.CostEstimate(flops=flops, bytes_accessed=nbytes, transcendentals=0)


def lanes_sum(v):
    width = v.shape[1]
    lane = lax.broadcasted_iota(jnp.int32, v.shape, 1)
    left = jnp.where(lane == 0, 0.0, pltpu.roll(v, 1, 1))
    right = jnp.where(lane == width - 1, 0.0, pltpu.roll(v, width - 1, 1))
    return left + right


def rows_sum(v, before, after):
    rows = v.shape[0]
    row = lax.broadcasted_iota(jnp.int32, v.shape, 0)
    up = jnp.where(row == 0, before, pltpu.roll(v, 1, 0))
    down = jnp.where(row == rows - 1, after, pltpu.roll(v, rows - 1, 0))
    return up + down


def pair_kernel(slot_ref, k_ref, a_ref, b_ref, c_ref, sum_ref, low_ref, high_ref):
    step = pl.program_id(0)
    members = a_ref.shape[0]

    @pl.when(step == 0)
    def _():
        sum_ref[...] = jnp.zeros_like(sum_ref)

    for m in range(members):
        slot = slot_ref[step * members + m]
        for level, ref in enumerate((a_ref, b_ref, c_ref)):
            sum_ref[level, slot] += ref[m, 0]

    @pl.when(step == pl.num_programs(0) - 1)
    def _():
        rank = sum_ref.shape[1]
        for s in range(rank):
            for part, (level, lo, hi) in enumerate(((1, 0, 7), (2, 0, 7), (2, 1, 6))):
                at = part * rank + s
                low_ref[at : at + 1, :] = sum_ref[level, s, lo : lo + 1, :]
                high_ref[at : at + 1, :] = sum_ref[level, s, hi : hi + 1, :]
        for level in range(k_ref.shape[0]):
            at = 3 * rank + level
            low_ref[at : at + 1, :] = k_ref[level, 0:1, :]
            high_ref[at : at + 1, :] = k_ref[level, 7:8, :]


def pair_sums(prior, slots, k, rank):
    members, levels, rows, width = prior.shape
    block = 4
    specs = [
        pl.BlockSpec((block, 1, rows, width), lambda i, s, l=l: (i, l, 0, 0))
        for l in (levels - 3, levels - 2, levels - 1)
    ]
    edge = 3 * rank + levels
    return pl.pallas_call(
        pair_kernel,
        grid_spec=pltpu.PrefetchScalarGridSpec(
            num_scalar_prefetch=1,
            grid=(members // block,),
            in_specs=[pl.BlockSpec((levels, rows, width), lambda i, s: (0, 0, 0))] + specs,
            out_specs=[
                pl.BlockSpec((3, rank, rows, width), lambda i, s: (0, 0, 0, 0)),
                pl.BlockSpec((edge, width), lambda i, s: (0, 0)),
                pl.BlockSpec((edge, width), lambda i, s: (0, 0)),
            ],
        ),
        out_shape=[shape(3, rank, rows, width), shape(edge, width), shape(edge, width)],
        compiler_params=pltpu.CompilerParams(vmem_limit_bytes=32 << 20),
        cost_estimate=cost(6 << 20),
        name="pair_sums",
    )(slots, k, prior, prior, prior)


def pack_kernel(u_ref, low_ref, high_ref):
    members = u_ref.shape[0] // 64
    for m in range(members):
        for r in range(2):
            for l in range(8):
                at = m * 64 + l * 8
                low_ref[m, r, l : l + 1, :] = u_ref[at + r : at + r + 1, :]
                high_ref[m, r, l : l + 1, :] = u_ref[at + 7 - r : at + 8 - r, :]


def pack(flat, first, count):
    width = flat.shape[1]
    block = 4
    out = pl.BlockSpec((block, 2, 8, width), lambda i: (i, 0, 0, 0))
    return pl.pallas_call(
        pack_kernel,
        grid=(count // block,),
        in_specs=[pl.BlockSpec((block * 64, width), lambda i: (first // block + i, 0))],
        out_specs=[out, out],
        out_shape=[shape(count, 2, 8, width)] * 2,
        compiler_params=pltpu.CompilerParams(vmem_limit_bytes=32 << 20),
        cost_estimate=cost(count * 3 * 128 << 10),
        name="pack_edges",
    )(flat)


def step_kernel(u_ref, before_ref, after_ref, first_ref, last_ref, k_ref, kb_ref, ka_ref, *rest):
    out_ref, one_ref = rest[-2:]
    levels = 8

    def edge(near, far, inner, k):
        zero = jnp.zeros((1, near.shape[1]), F32)
        total = rows_sum(near, zero, zero) + lanes_sum(near) + far + inner
        return near + k * (total - 6.0 * near)

    b0, a0 = before_ref[0, 0], after_ref[0, 0]
    b1 = edge(b0, before_ref[0, 1], first_ref[0, 0], kb_ref[...])
    a1 = edge(a0, after_ref[0, 1], last_ref[0, 0], ka_ref[...])

    def sweep(src, dst, before, after):
        for l in range(levels):
            v = src[l * 8 : l * 8 + 8, :]
            total = rows_sum(v, before[l : l + 1, :], after[l : l + 1, :]) + lanes_sum(v)
            if l > 0:
                total = total + src[l * 8 - 8 : l * 8, :]
            if l < levels - 1:
                total = total + src[l * 8 + 8 : l * 8 + 16, :]
            dst[l * 8 : l * 8 + 8, :] = v + k_ref[l] * (total - 6.0 * v)

    sweep(u_ref, one_ref, b0, a0)
    sweep(one_ref, out_ref, b1, a1)


def two_steps(flat, before, after, low, high, k, kb, ka, done, first):
    count, _, levels, width = before.shape
    rows = 64
    edge = pl.BlockSpec((1, 2, levels, width), lambda i: (i, 0, 0, 0))
    inner = pl.BlockSpec((1, 1, levels, width), lambda i: (i, 0, 0, 0))
    small = pl.BlockSpec((levels, width), lambda i: (0, 0))
    place = pl.BlockSpec((rows, width), lambda i: (first + i, 0))
    operands = [flat, before, after, low, high, k, kb, ka]
    specs = [place, edge, edge, inner, inner, pl.BlockSpec((levels, 8, width), lambda i: (0, 0, 0)), small, small]
    aliases = {}
    if done is not None:
        operands.append(done)
        specs.append(pl.BlockSpec(memory_space=pl.ANY))
        aliases = {8: 0}
    return pl.pallas_call(
        step_kernel,
        grid=(count,),
        in_specs=specs,
        out_specs=place,
        out_shape=shape(*flat.shape),
        scratch_shapes=[pltpu.VMEM((rows, width), F32)],
        input_output_aliases=aliases,
        compiler_params=pltpu.CompilerParams(vmem_limit_bytes=32 << 20),
        cost_estimate=cost(count * 640 << 10),
        name="two_steps",
    )(*operands)


def surface_kernel(p_ref, before_ref, after_ref, low_ref, high_ref, k_ref, out_ref):
    rank = p_ref.shape[1] // 8
    width = p_ref.shape[2]
    levels = k_ref.shape[0]
    zero = jnp.zeros((1, width), F32)

    def edge(ref, own_ref):
        low, near, far = (ref[i * rank : (i + 1) * rank, :] for i in range(3))
        k = ref[3 * rank + levels - 1 : 3 * rank + levels, :]
        inner = own_ref[rank : 2 * rank, :]
        return near + k * (low + far + inner + lanes_sum(near) - 6.0 * near)

    b1, a1 = edge(before_ref, low_ref), edge(after_ref, high_ref)
    k6, k7 = k_ref[levels - 2], k_ref[levels - 1]
    piece = out_ref.shape[2]
    for s in range(rank):
        at = pl.ds(s * 8, 8)
        u5, u6, u7 = (p_ref[i, at, :] for i in range(3))

        def row(ref, part):
            return ref[part * rank + s : part * rank + s + 1, :]

        t6 = rows_sum(u6, row(before_ref, 0), row(after_ref, 0)) + lanes_sum(u6) + u5 + u7
        t7 = rows_sum(u7, row(before_ref, 1), row(after_ref, 1)) + lanes_sum(u7) + u6
        v6 = u6 + k6 * (t6 - 6.0 * u6)
        v7 = u7 + k7 * (t7 - 6.0 * u7)
        total = rows_sum(v7, b1[s : s + 1, :], a1[s : s + 1, :]) + lanes_sum(v7) + v6
        w7 = v7 + k7 * (total - 6.0 * v7)
        for g in range(width // piece):
            out_ref[g, s * 8 : s * 8 + 8, :] = w7[:, g * piece : (g + 1) * piece]


def surface(sums, before, after, low, high, k, groups):
    levels, rank, rows, width = sums.shape
    return pl.pallas_call(
        surface_kernel,
        in_specs=[VMEM] * 6,
        out_specs=VMEM,
        out_shape=shape(groups, rank * rows, width // groups),
        compiler_params=pltpu.CompilerParams(vmem_limit_bytes=32 << 20),
        cost_estimate=cost(4 << 20),
        name="surface_steps",
    )(sums.reshape(levels, rank * rows, width), before, after, low, high, k)


def sensor_kernel(at_ref, cell_ref, value_ref, var_ref, out_ref):
    width, columns = 1024, out_ref.shape[1]
    rows = out_ref.shape[0] // 2
    chunks, span = cell_ref.shape
    weight = 1.0 / var_ref[...]
    local = cell_ref[...] - at_ref[0] * (rows * width)
    x = local // width
    y = local - x * width - at_ref[1] * columns
    left, right = [], []
    row = lax.broadcasted_iota(jnp.int32, (rows, span), 0)
    column = lax.broadcasted_iota(jnp.int32, (columns, span), 0)
    weighted = weight * value_ref[...]
    for c in range(chunks):
        hit = x[c : c + 1, :] == row
        left.append(
            jnp.concatenate(
                [jnp.where(hit, weight[c : c + 1, :], 0.0), jnp.where(hit, weighted[c : c + 1, :], 0.0)], 0
            )
        )
        right.append(jnp.where(y[c : c + 1, :] == column, 1.0, 0.0))
    out_ref[...] = lax.dot_general(
        jnp.concatenate(left, 1),
        jnp.concatenate(right, 1),
        (((1,), (1,)), ((), ())),
        precision=HI,
        preferred_element_type=F32,
    )


def sensors(place, cells, values, var, columns):
    return pl.pallas_call(
        sensor_kernel,
        in_specs=[SMEM, VMEM, VMEM, VMEM],
        out_specs=VMEM,
        out_shape=shape(16, columns),
        compiler_params=pltpu.CompilerParams(vmem_limit_bytes=32 << 20),
        cost_estimate=cost(4 << 20),
        name="sensor_sums",
    )(place, *(a.reshape(-1, 128) for a in (cells, values, var)))


def gram_kernel(place_ref, obs_ref, own_ref, r1_ref, r2_ref, r3_ref, sums_ref, s_ref, mean_ref, raw_ref):
    chip, core = place_ref[1] // 2, place_ref[1] % 2
    for d, ref in ((0, own_ref), (1, r1_ref), (2, r2_ref), (3, r3_ref)):
        for slot in range(2):
            group = jnp.bitwise_xor(chip, d) * 2 + jnp.bitwise_xor(core, slot)
            raw_ref[pl.ds(pl.multiple_of(group * 128, 128), 128), :] = ref[slot]
    total = None
    sketches = raw_ref.shape[0] // 8
    member_total = 2 * sketches
    for x in range(0, 8, 2):
        both, means, weights, values = [], [], [], []
        for i in (x, x + 1):
            raw = raw_ref[pl.ds(i, sketches, stride=8), :]
            mean = jnp.sum(raw, axis=0, keepdims=True) * (1.0 / member_total)
            dev = raw - 2.0 * mean
            s_ref[:, i * 128 : (i + 1) * 128] = dev
            mean_ref[i : i + 1, :] = mean
            both.append(dev)
            w = obs_ref[i : i + 1, :]
            weights.append(w)
            values.append(obs_ref[8 + i : 9 + i, :] - mean * w)
        dev = jnp.concatenate(both, 1)
        w = jnp.concatenate(weights, 1)
        z = jnp.broadcast_to(jnp.concatenate(values, 1), (8, dev.shape[1]))
        left = jnp.concatenate([dev, dev * w, z], 0)
        part = lax.dot_general(left, dev, (((1,), (1,)), ((), ())), precision=HI, preferred_element_type=F32)
        total = part if total is None else total + part
    gram, weighted, rhs = total[:sketches], total[sketches : 2 * sketches], total[2 * sketches :]
    row = lax.broadcasted_iota(jnp.int32, gram.shape, 0)
    lane = lax.broadcasted_iota(jnp.int32, gram.shape, 1)
    sums_ref[0:sketches, :] = jnp.where(lane > row, gram, weighted)
    sums_ref[sketches : sketches + 8, :] = jnp.broadcast_to(
        jnp.sum(jnp.where(lane == row, gram, 0.0), axis=0, keepdims=True), (8, 128)
    )
    sums_ref[sketches + 8 : sketches + 16, :] = rhs


def gram(place, obs, own, r1, r2, r3):
    return pl.pallas_call(
        gram_kernel,
        in_specs=[SMEM] + [VMEM] * 5,
        out_specs=[VMEM] * 3,
        out_shape=[shape(144, 128), shape(128, 1024), shape(8, 128)],
        scratch_shapes=[pltpu.VMEM((1024, 128), F32)],
        compiler_params=pltpu.CompilerParams(vmem_limit_bytes=32 << 20),
        cost_estimate=cost(4 << 20),
        name="gram_sums",
    )(place, obs, own, r1, r2, r3)


def dot(a, b, ca=1, cb=0):
    return lax.dot_general(a, b, (((ca,), (cb,)), ((), ())), precision=HI, preferred_element_type=F32)


def analysis_kernel(sums_ref, m_ref, s_ref, mean_ref, out_ref):
    n = 128
    rank = m_ref.shape[2]
    packed = sums_ref[0:n, :]
    row = lax.broadcasted_iota(jnp.int32, (n, n), 0)
    lane = lax.broadcasted_iota(jnp.int32, (n, n), 1)
    upper = jnp.where(lane > row, packed, 0.0)
    lower = jnp.where(lane < row, packed, 0.0)
    g = upper + upper.T + jnp.where(lane == row, sums_ref[n : n + 1, :], 0.0)
    h = lower + lower.T + jnp.where(lane == row, packed, 0.0)
    q = sums_ref[n + 8 : n + 9, :]

    def mixer(level, blocks):
        mt = m_ref[level].T
        rows = []
        for p in range(blocks):
            parts = [jnp.zeros((rank, 2 * rank), F32)] * blocks
            parts[p] = mt
            rows.append(jnp.concatenate(parts, 1) if blocks > 1 else mt)
        return jnp.concatenate(rows, 0) if blocks > 1 else rows[0]

    def eliminate(c, extra, blocks):
        wide = c.shape[1]
        both = jnp.concatenate([c, extra], 1)
        width = both.shape[1]
        sub = lax.broadcasted_iota(jnp.int32, (rank, width), 0)
        parts = [both[b * rank : (b + 1) * rank, :] for b in range(blocks)]
        for j in range(rank - 1):
            for b in range(blocks):
                v = parts[b]
                at = b * rank + j
                column = jnp.broadcast_to(v[:, at : at + 1], v.shape)
                factor = jnp.where(sub > j, column / column[j : j + 1, :], 0.0)
                parts[b] = v - factor * v[j : j + 1, :]
        both = jnp.concatenate(parts, 0) if blocks > 1 else parts[0]
        return both[:, :wide], both[:, wide:]

    def eye(k):
        return jnp.where(
            lax.broadcasted_iota(jnp.int32, (k, k), 0) == lax.broadcasted_iota(jnp.int32, (k, k), 1), 1.0, 0.0
        ).astype(F32)

    blocks = n // rank
    c = g
    w = None
    for level in range(m_ref.shape[0]):
        tc, t = eliminate(c, eye(c.shape[0]), blocks)
        blocks //= 2
        mix = mixer(level, blocks)
        x = dot(mix, t)
        c = dot(dot(mix, tc), x, 1, 1)
        w = x if w is None else dot(x, w)
    h3 = dot(dot(w, h), w, 1, 1)
    q3 = jnp.sum(w * q, axis=1, keepdims=True)
    u, t3 = eliminate(c, eye(rank), 1)
    system = 255.0 * eye(rank) + dot(dot(t3, h3), t3, 1, 1)
    rhs = jnp.sum(t3 * dot(jnp.broadcast_to(q, (8, n)), w, 1, 1)[0:1, :], axis=1, keepdims=True)
    v = jnp.concatenate([system, jnp.broadcast_to(rhs, (rank, rank))], 1)
    sub = lax.broadcasted_iota(jnp.int32, v.shape, 0)
    for j in range(rank):
        column = jnp.broadcast_to(v[:, j : j + 1], v.shape)
        factor = jnp.where(sub != j, column / column[j : j + 1, :], 0.0)
        v = v - factor * v[j : j + 1, :]
    diagonal = jnp.sum(jnp.where(eye(rank) > 0.5, v[:, :rank], 0.0), axis=1, keepdims=True)
    coef = v[:, rank : rank + 1] / diagonal
    basis_map = dot(t3, w)
    weights = jnp.sum(coef * basis_map, axis=0, keepdims=True)
    increment = dot(jnp.broadcast_to(weights, (8, n)), s_ref[...])
    for i in range(8):
        out_ref[i : i + 1, :] = mean_ref[i : i + 1, :] + increment[0:1, i * 128 : (i + 1) * 128]


def analysis(sums, merge, s, mean):
    return pl.pallas_call(
        analysis_kernel,
        in_specs=[VMEM] * 4,
        out_specs=VMEM,
        out_shape=shape(8, 128),
        compiler_params=pltpu.CompilerParams(vmem_limit_bytes=32 << 20),
        cost_estimate=cost(16 << 20),
        name="analysis",
    )(sums, merge, s, mean)


def to_next(v):
    size = lax.axis_size("tile")
    return lax.ppermute(v, "tile", [(i, i + 1) for i in range(size - 1)])


def to_previous(v):
    size = lax.axis_size("tile")
    return lax.ppermute(v, "tile", [(i + 1, i) for i in range(size - 1)])


def across(v, axis, bits):
    return lax.ppermute(v, axis, [(i, i ^ bits) for i in range(lax.axis_size(axis))])


def local(prior, k, slots, merge, cells, values, var):
    members, levels, rows, width = prior.shape
    rank = merge.shape[2]
    groups = lax.axis_size("grp")
    tile, group = lax.axis_index("tile"), lax.axis_index("grp")
    chip, core = group // 2, group % 2
    place = jnp.stack([tile, group]).astype(jnp.int32)
    flat = prior.reshape(members * levels * rows, width)

    sums, low, high = pair_sums(prior, slots, k, rank)
    before = to_next(high)
    after = to_previous(low)
    kb, ka = before[3 * rank :], after[3 * rank :]

    arrived = []
    first = 0
    for count in CHUNKS:
        lo, hi = pack(flat, first, count)
        arrived.append((first, to_next(hi), to_previous(lo), lo, hi))
        first += count

    pieces = surface(sums, before, after, low, high, k, groups).reshape(groups // 2, 2, rank * rows, width // groups)
    obs = sensors(place, cells, values, var, width // groups)

    mine = lax.dynamic_index_in_dim(pieces, core, 1, False)
    other = lax.dynamic_index_in_dim(pieces, 1 - core, 1, False)
    pairs = jnp.stack([mine, across(other, "grp", 1)], 1)

    def pair_for(bits):
        return lax.dynamic_index_in_dim(pairs, chip ^ bits, 0, False)

    own = pair_for(0)
    r1, r3, r2 = (across(pair_for(bits), "grp", 2 * bits) for bits in (1, 3, 2))
    part, sketches, mean = gram(place, obs, own, r1, r2, r3)

    half = part.reshape(2, -1, part.shape[1])
    total = lax.dynamic_index_in_dim(half, core, 0, False) + across(
        lax.dynamic_index_in_dim(half, 1 - core, 0, False), "grp", 1
    )
    for axis, bits in (("grp", 2), ("grp", 6), ("tile", 4), ("tile", 12), ("tile", 1), ("tile", 3)):
        total = total + across(total, axis, bits)
    second = across(total, "grp", 1)
    both = jnp.where(core == 0, jnp.concatenate([total, second], 0), jnp.concatenate([second, total], 0))

    posterior = analysis(both, merge, sketches, mean)

    out = None
    for first, b, a, lo, hi in arrived:
        out = two_steps(flat, b, a, lo, hi, k, kb, ka, out, first)
    return out.reshape(prior.shape), posterior


def solution(mesh):
    in_specs = (P("grp", None, "tile", None), P(None, "tile", None), P("grp"), P(), P(), P(), P())
    out_specs = (P("grp", None, "tile", None), P("tile", "grp"))
    return jax.shard_map(local, mesh=mesh, in_specs=in_specs, out_specs=out_specs, check_vma=False)
```

```python
import functools

import jax
import jax.numpy as jnp
from jax import lax
from jax.experimental import pallas as pl
from jax.experimental.pallas import tpu as pltpu
from jax.sharding import PartitionSpec as P

HI = lax.Precision.HIGHEST
VMEM = pl.BlockSpec(memory_space=pltpu.VMEM)
SMEM = pl.BlockSpec(memory_space=pltpu.SMEM)
ANY = pl.BlockSpec(memory_space=pl.ANY)
HBM = pl.BlockSpec(memory_space=pltpu.HBM)
ROWS = 8
LIMIT = 16 << 20
LARGE = 105 << 19
CHUNKS = (2, 2)
F32 = jnp.float32


def shape(*dims):
    return jax.ShapeDtypeStruct(dims, F32)


def cost(nbytes, flops=0):
    return pl.CostEstimate(flops=flops, bytes_accessed=nbytes, transcendentals=0)


def params(limit=LIMIT):
    return pltpu.CompilerParams(vmem_limit_bytes=limit)


def lanes_sum(v):
    tiles = [v[:, t : t + 128] for t in range(0, v.shape[1], 128)]
    lane = lax.broadcasted_iota(jnp.int32, tiles[0].shape, 1)
    first, last = lane == 0, lane == 127
    ups = [jnp.zeros_like(tiles[0])] + [pltpu.roll(t, 1, 1) for t in tiles]
    downs = [pltpu.roll(t, 127, 1) for t in tiles] + [jnp.zeros_like(tiles[0])]
    out = [
        jnp.where(first, ups[t], ups[t + 1]) + jnp.where(last, downs[t + 1], downs[t])
        for t in range(len(tiles))
    ]
    return jnp.concatenate(out, 1)


def pair_kernel(slot_ref, k_ref, u_ref, sum_ref, low_ref, high_ref, pair_ref, seen_ref, order_ref, sem, k_sem):
    members, levels = u_ref.shape[:2]
    rank = sum_ref.shape[2]
    at = pl.ds(3 * rank, levels)
    turned = [
        pltpu.make_async_copy(k_ref.at[:, 0, :], low_ref.at[at], k_sem.at[0]),
        pltpu.make_async_copy(k_ref.at[:, ROWS - 1, :], high_ref.at[at], k_sem.at[1]),
    ]
    for copy in turned:
        copy.start()
    for s in range(rank):
        seen_ref[s] = 0

    def place(m, carry):
        s = slot_ref[m]
        which = jnp.minimum(seen_ref[s], 1)
        order_ref[2 * s + which] = m
        seen_ref[s] = which + 1
        return carry

    lax.fori_loop(0, members, place, 0)
    copies = [
        pltpu.make_async_copy(
            u_ref.at[order_ref[2 * s + i], pl.ds(levels - 3, 3)], pair_ref.at[i, :, :, s, :], sem.at[i, s]
        )
        for s in range(rank)
        for i in range(2)
    ]
    for copy in copies:
        copy.start()
    for copy in turned + copies:
        copy.wait()
    for l in range(3):
        for x in range(ROWS):
            sum_ref[l, x] = pair_ref[0, l, x] + pair_ref[1, l, x]
    for part, (level, x) in enumerate(((1, 0), (2, 0), (2, 1))):
        at = pl.ds(part * rank, rank)
        low_ref[at, :] = sum_ref[level, x]
        high_ref[at, :] = sum_ref[level, ROWS - 1 - x]


def pair_sums(prior, slots, k, rank):
    members, levels, rows, width = prior.shape
    edge = 3 * rank + levels
    return pl.pallas_call(
        pair_kernel,
        in_specs=[SMEM, HBM, HBM],
        out_specs=[VMEM] * 3,
        out_shape=[
            shape(3, rows, rank, width),
            shape(edge, width),
            shape(edge, width),
        ],
        scratch_shapes=[
            pltpu.VMEM((2, 3, rows, rank, width), F32),
            pltpu.SMEM((rank,), jnp.int32),
            pltpu.SMEM((members,), jnp.int32),
            pltpu.SemaphoreType.DMA((2, rank)),
            pltpu.SemaphoreType.DMA((2,)),
        ],
        compiler_params=params(54 << 20),
        cost_estimate=cost(6 << 20),
        name="pair_sums",
    )(slots, k, prior)


def pack_kernel(first, u_ref, *rest):
    low_ref, high_ref, sem = rest[-3:]
    groups, depth, _, span, _ = low_ref.shape
    copies = []
    for g in range(groups):
        for m in range(span):
            for r in range(depth):
                for side, (ref, x) in enumerate(((low_ref, r), (high_ref, ROWS - 1 - r))):
                    copies.append(
                        pltpu.make_async_copy(
                            u_ref.at[first + g * span + m, :, x, :], ref.at[g, r, :, m, :], sem.at[g, m, r, side]
                        )
                    )
    for copy in copies:
        copy.start()
    for copy in copies:
        copy.wait()


def pack(prior, first, groups, *tokens):
    levels, width = prior.shape[1], prior.shape[3]
    return pl.pallas_call(
        functools.partial(pack_kernel, first),
        in_specs=[HBM] + [ANY] * len(tokens),
        out_specs=[VMEM] * 2,
        out_shape=[shape(groups, 2, levels, 8, width)] * 2,
        scratch_shapes=[pltpu.SemaphoreType.DMA((groups, 8, 2, 2))],
        compiler_params=params(LARGE),
        cost_estimate=cost(groups << 21),
        name="pack_edges",
    )(prior, *tokens)


def step_kernel(first, u_ref, before_ref, after_ref, k_ref, kb_ref, ka_ref, *rest):
    out_ref, token_ref, u, v, w, in_sem, edge_sem, out_sem = rest[-8:]
    token_ref[...] = jnp.zeros_like(token_ref)
    levels, span, width = u_ref.shape[1], u.shape[3], u.shape[4]
    groups = before_ref.shape[0]
    part = levels // 4

    def fetch(g, p):
        slot = g % 2
        at, to = pl.ds(p * part, part), pl.ds(p * part + 1, part)
        copies = [
            pltpu.make_async_copy(
                u_ref.at[first + g * span + m, at], u.at[slot, to, pl.ds(2, ROWS), m, :], in_sem.at[slot, p, m]
            )
            for m in range(span)
        ]
        for r in range(2):
            for side, (ref, x) in enumerate(((before_ref, 1 - r), (after_ref, ROWS + 2 + r))):
                copies.append(
                    pltpu.make_async_copy(ref.at[g, r, at], u.at[slot, to, x], edge_sem.at[slot, p, r, side])
                )
        return copies

    def store(g, p):
        slot, at = g % 2, pl.ds(p * part, part)
        return [
            pltpu.make_async_copy(
                w.at[slot, at, :, m, :], out_ref.at[first + g * span + m, at], out_sem.at[slot, p, m]
            )
            for m in range(span)
        ]

    parts = levels // part
    for p in range(parts):
        for copy in fetch(0, p):
            copy.start()
    zero = jnp.zeros((span, width), F32)
    for l in (0, levels + 1):
        for x in range(ROWS + 4):
            for slot in range(u.shape[0]):
                u[slot, l, x] = zero
        for x in range(ROWS + 2):
            v[l, x] = zero
    tile = (span, 128)
    lane = lax.broadcasted_iota(jnp.int32, tile, 1)
    left, right = lane == 0, lane == 127

    def tiles(ref, l, x):
        return [ref[l, x, :, t : t + 128] for t in range(0, width, 128)]

    def one_step(src, l, x, rows, k):
        blank = jnp.zeros(tile, F32)
        before, here, after = rows
        ups = [blank] + [pltpu.roll(h, 1, 1) for h in here]
        downs = [pltpu.roll(h, 127, 1) for h in here] + [blank]
        out = []
        for t, h in enumerate(here):
            cut = pl.ds(t * 128, 128)
            total = (before[t] + after[t]) + (src[l - 1, x, :, cut] + src[l + 1, x, :, cut])
            total += jnp.where(left, ups[t], ups[t + 1]) + jnp.where(right, downs[t + 1], downs[t])
            out.append(h + k[:, t * 128 : t * 128 + 128] * (total - 6.0 * h))
        return out

    for g in range(groups):
        slot = g % 2
        if g + 1 < groups:
            for p in range(parts):
                for copy in fetch(g + 1, p):
                    copy.start()
        if g >= 2:
            for p in range(parts):
                for copy in store(g - 2, p):
                    copy.wait()

        def first_step(l):
            rows = [tiles(u.at[slot], l + 1, x) for x in range(2)]
            for x in range(-1, ROWS + 1):
                rows = rows[-2:] + [tiles(u.at[slot], l + 1, x + 3)]
                if x < 0:
                    k = kb_ref[l : l + 1, :]
                elif x == ROWS:
                    k = ka_ref[l : l + 1, :]
                else:
                    k = k_ref[l, x : x + 1, :]
                for t, tile_out in enumerate(one_step(u.at[slot], l + 1, x + 2, rows, k)):
                    v[l + 1, x + 1, :, t * 128 : t * 128 + 128] = tile_out

        def second_step(l):
            rows = [tiles(v, l + 1, x) for x in range(2)]
            for x in range(ROWS):
                rows = rows[-2:] + [tiles(v, l + 1, x + 2)]
                for t, tile_out in enumerate(one_step(v, l + 1, x + 1, rows, k_ref[l, x : x + 1, :])):
                    w[slot, l, x, :, t * 128 : t * 128 + 128] = tile_out

        for copy in fetch(g, 0):
            copy.wait()
        first_step(0)
        done = 0
        for p in range(parts):
            if p + 1 < parts:
                for copy in fetch(g, p + 1):
                    copy.wait()
            top = (p + 1) * part if p + 1 < parts else levels - 1
            for l in range(done + 1, top + 1):
                first_step(l)
                second_step(l - 1)
            done = top
            if p + 1 < parts:
                for copy in store(g, p):
                    copy.start()
        second_step(levels - 1)
        for copy in store(g, parts - 1):
            copy.start()
    for g in range(max(groups - 2, 0), groups):
        for p in range(parts):
            for copy in store(g, p):
                copy.wait()


def two_steps(prior, before, after, k, kb, ka, done, first, *tokens):
    members, levels, rows, width = prior.shape
    slots = min(before.shape[0], 2)
    operands = [prior, before, after, k, kb, ka]
    specs = [HBM] + [ANY] * 2 + [VMEM] * 3
    aliases = {}
    if done is not None:
        operands.append(done)
        specs.append(HBM)
        aliases = {6: 0}
    return pl.pallas_call(
        functools.partial(step_kernel, first),
        in_specs=specs + [ANY] * len(tokens),
        out_specs=[HBM, VMEM],
        out_shape=[shape(*prior.shape), shape(8, 128)],
        scratch_shapes=[
            pltpu.VMEM((slots, levels + 2, rows + 4, 8, width), F32),
            pltpu.VMEM((levels + 2, rows + 2, 8, width), F32),
            pltpu.VMEM((slots, levels, rows, 8, width), F32),
            pltpu.SemaphoreType.DMA((slots, 4, 8)),
            pltpu.SemaphoreType.DMA((slots, 4, 2, 2)),
            pltpu.SemaphoreType.DMA((slots, 4, 8)),
        ],
        input_output_aliases=aliases,
        compiler_params=params(LARGE),
        cost_estimate=cost(before.shape[0] << 23),
        name="two_steps",
    )(*operands, *tokens)


def surface_kernel(p_ref, before_ref, after_ref, k_ref, *rest):
    out_ref = rest[-1]
    rank = p_ref.shape[2]
    top = before_ref.shape[0] - 1

    def edge(ref, x):
        low, near, far = (ref[i * rank : (i + 1) * rank, :] for i in range(3))
        k = ref[top : top + 1, :]
        return near + k * (low + far + p_ref[2, x] + lanes_sum(near) - 6.0 * near)

    v6, v7 = [], [edge(before_ref, 0)]
    for x in range(ROWS):
        u6, u7 = p_ref[1, x], p_ref[2, x]

        def beside(level, part):
            before = p_ref[level, x - 1] if x > 0 else before_ref[part * rank : (part + 1) * rank, :]
            after = p_ref[level, x + 1] if x < ROWS - 1 else after_ref[part * rank : (part + 1) * rank, :]
            return before + after

        v6.append(u6 + k_ref[0, x : x + 1, :] * (beside(1, 0) + lanes_sum(u6) + p_ref[0, x] + u7 - 6.0 * u6))
        v7.append(u7 + k_ref[1, x : x + 1, :] * (beside(2, 1) + lanes_sum(u7) + u6 - 6.0 * u7))
    v7.append(edge(after_ref, ROWS - 1))
    piece = out_ref.shape[3]
    for x in range(ROWS):
        here = v7[x + 1]
        total = v7[x] + v7[x + 2] + lanes_sum(here) + v6[x]
        out = here + k_ref[1, x : x + 1, :] * (total - 6.0 * here)
        for g in range(out_ref.shape[0]):
            out_ref[g, x] = out[:, g * piece : (g + 1) * piece]


def surface(sums, before, after, k, groups, *tokens):
    _, rows, rank, width = sums.shape
    levels = k.shape[0]
    edge = pl.BlockSpec(before.shape, lambda i: (0, 0))
    return pl.pallas_call(
        surface_kernel,
        grid=(1,),
        in_specs=[
            pl.BlockSpec(sums.shape, lambda i: (0, 0, 0, 0)),
            edge,
            edge,
            pl.BlockSpec((2, rows, width), lambda i: (levels // 2 - 1, 0, 0)),
        ]
        + [ANY] * len(tokens),
        out_specs=pl.BlockSpec((groups, rows, rank, width // groups), lambda i: (0, 0, 0, 0)),
        out_shape=shape(groups, rows, rank, width // groups),
        compiler_params=params(),
        cost_estimate=cost(4 << 20),
        name="surface_steps",
    )(sums, before, after, k, *tokens)


def sensor_kernel(at_ref, cell_ref, value_ref, var_ref, m_ref, *rest):
    rank = m_ref.shape[2]
    out_ref, *mix_refs = rest[-1 - m_ref.shape[0] :]
    for level, ref in enumerate(mix_refs):
        ref[...] = jnp.zeros_like(ref)
        turned = m_ref[level].T
        for p in range(ref.shape[0] // rank):
            ref[p * rank : (p + 1) * rank, 2 * p * rank : 2 * (p + 1) * rank] = turned
    width, columns = 1024, out_ref.shape[1]
    rows = out_ref.shape[0] // 2
    chunks, span = cell_ref.shape
    weight = 1.0 / var_ref[...]
    local = cell_ref[...] - at_ref[0] * (rows * width)
    x = local // width
    y = local - x * width - at_ref[1] * columns
    left, right = [], []
    row = lax.broadcasted_iota(jnp.int32, (rows, span), 0)
    column = lax.broadcasted_iota(jnp.int32, (columns, span), 0)
    weighted = weight * value_ref[...]
    for c in range(chunks):
        hit = x[c : c + 1, :] == row
        left.append(
            jnp.concatenate(
                [jnp.where(hit, weight[c : c + 1, :], 0.0), jnp.where(hit, weighted[c : c + 1, :], 0.0)], 0
            )
        )
        right.append(jnp.where(y[c : c + 1, :] == column, 1.0, 0.0))
    out_ref[...] = lax.dot_general(
        jnp.concatenate(left, 1),
        jnp.concatenate(right, 1),
        (((1,), (1,)), ((), ())),
        precision=HI,
        preferred_element_type=F32,
    )


def sensors(place, cells, values, var, merge, columns, *tokens):
    rank = merge.shape[2]
    mixers = [shape(rank << i, 2 * rank << i) for i in range(merge.shape[0])][::-1]
    return pl.pallas_call(
        sensor_kernel,
        in_specs=[SMEM] + [VMEM] * 4 + [ANY] * len(tokens),
        out_specs=[VMEM] * (1 + len(mixers)),
        out_shape=[shape(16, columns)] + mixers,
        compiler_params=params(),
        cost_estimate=cost(4 << 20),
        name="sensor_sums",
    )(place, *(a.reshape(-1, 128) for a in (cells, values, var)), merge, *tokens)


def gram_kernel(place_ref, obs_ref, own_ref, r1_ref, r2_ref, r3_ref, *rest):
    sums_ref, s_ref, mean_ref, raw_ref = rest[-4:]
    chip, core = place_ref[1] // 2, place_ref[1] % 2
    for d, ref in ((0, own_ref), (1, r1_ref), (2, r2_ref), (3, r3_ref)):
        for slot in range(2):
            group = jnp.bitwise_xor(chip, d) * 2 + jnp.bitwise_xor(core, slot)
            rank = ref.shape[2]
            at = pl.ds(pl.multiple_of(group * rank, rank), rank)
            for x in range(ROWS):
                raw_ref[x, at, :] = ref[slot, x]
    total = None
    sketches = raw_ref.shape[1]
    member_total = 2 * sketches
    for x in range(0, 8, 2):
        both, means, weights, values = [], [], [], []
        for i in (x, x + 1):
            raw = raw_ref[i]
            mean = jnp.sum(raw, axis=0, keepdims=True) * (1.0 / member_total)
            dev = raw - 2.0 * mean
            s_ref[:, i * 128 : (i + 1) * 128] = dev
            mean_ref[i : i + 1, :] = mean
            both.append(dev)
            w = obs_ref[i : i + 1, :]
            weights.append(w)
            values.append(obs_ref[8 + i : 9 + i, :] - mean * w)
        dev = jnp.concatenate(both, 1)
        w = jnp.concatenate(weights, 1)
        z = jnp.broadcast_to(jnp.concatenate(values, 1), (8, dev.shape[1]))
        left = jnp.concatenate([dev, dev * w, z], 0)
        part = lax.dot_general(left, dev, (((1,), (1,)), ((), ())), precision=HI, preferred_element_type=F32)
        total = part if total is None else total + part
    gram, weighted, rhs = total[:sketches], total[sketches : 2 * sketches], total[2 * sketches :]
    row = lax.broadcasted_iota(jnp.int32, gram.shape, 0)
    lane = lax.broadcasted_iota(jnp.int32, gram.shape, 1)
    sums_ref[0:sketches, :] = jnp.where(lane > row, gram, weighted)
    sums_ref[sketches : sketches + 8, :] = jnp.broadcast_to(
        jnp.sum(jnp.where(lane == row, gram, 0.0), axis=0, keepdims=True), (8, 128)
    )
    sums_ref[sketches + 8 : sketches + 16, :] = rhs


def gram(place, obs, own, r1, r2, r3, *tokens):
    return pl.pallas_call(
        gram_kernel,
        in_specs=[SMEM] + [VMEM] * 5 + [ANY] * len(tokens),
        out_specs=[VMEM] * 3,
        out_shape=[shape(144, 128), shape(128, 1024), shape(8, 128)],
        scratch_shapes=[pltpu.VMEM((8, 128, 128), F32)],
        compiler_params=params(),
        cost_estimate=cost(4 << 20),
        name="gram_sums",
    )(place, obs, own, r1, r2, r3, *tokens)


def dot(a, b, ca=1, cb=0):
    return lax.dot_general(a, b, (((ca,), (cb,)), ((), ())), precision=HI, preferred_element_type=F32)


def analysis_kernel(sums_ref, mix0_ref, mix1_ref, mix2_ref, s_ref, mean_ref, out_ref):
    n = 128
    mixers = (mix0_ref, mix1_ref, mix2_ref)
    rank = mix2_ref.shape[0]
    packed = sums_ref[0:n, :]
    row = lax.broadcasted_iota(jnp.int32, (n, n), 0)
    lane = lax.broadcasted_iota(jnp.int32, (n, n), 1)
    upper = jnp.where(lane > row, packed, 0.0)
    lower = jnp.where(lane < row, packed, 0.0)
    g = upper + upper.T + jnp.where(lane == row, sums_ref[n : n + 1, :], 0.0)
    h = lower + lower.T + jnp.where(lane == row, packed, 0.0)
    q = sums_ref[n + 8 : n + 9, :]

    block = (rank, n)
    sub = lax.broadcasted_iota(jnp.int32, block, 0)
    at = lax.broadcasted_iota(jnp.int32, block, 1)
    unit = jnp.where(at % rank == sub, 1.0, 0.0)

    def eliminate(d, extra, visit=None):
        columns = [jnp.take_along_axis(d, at // rank * rank + j, axis=1) for j in range(rank)]
        for j in range(rank):
            c = columns[j]
            inverse = 1.0 / c[j : j + 1, :]
            if visit is not None:
                visit(j, inverse, extra)
            if j == rank - 1:
                break
            factor = jnp.where(sub > j, c * inverse, 0.0)
            for k in range(j + 1, rank):
                columns[k] = columns[k] - factor * c[k : k + 1, :]
            extra = [e - factor * e[j : j + 1, :] for e in extra]
        return extra

    def widened(v):
        if v.shape[1] == n:
            return v
        return jnp.concatenate([v, jnp.zeros((rank, n - v.shape[1]), F32)], 1) + jnp.where(
            at >= v.shape[1], unit, 0.0
        )

    c = g
    w = None
    for mix_ref in mixers:
        size = c.shape[0]
        d = jnp.zeros((rank, size), F32)
        for b in range(size // rank):
            d = d + jnp.where(at[:, :size] // rank == b, c[b * rank : (b + 1) * rank, :], 0.0)
        (t,) = eliminate(widened(d), [unit])
        t = jnp.concatenate([t[:, :size]] * (size // rank), 0)
        t = jnp.where(row[:size, :size] // rank == lane[:size, :size] // rank, t, 0.0)
        x = dot(mix_ref[...], t)
        c = dot(dot(x, c), x, 1, 1)
        w = x if w is None else dot(x, w)
    h3 = dot(dot(w, h), w, 1, 1)
    (t3,) = eliminate(widened(c), [unit])
    t3 = t3[:, :rank]
    basis_map = dot(t3, w)
    eye = unit[:, :rank]
    system = 255.0 * eye + dot(dot(t3, h3), t3, 1, 1)
    rhs = jnp.broadcast_to(jnp.sum(basis_map * q, axis=1, keepdims=True), block)
    found = []

    def visit(j, inverse, extra):
        y, v = extra
        found.append((y[j : j + 1, :] * inverse[:, 0:1]) * v[j : j + 1, :])

    eliminate(jnp.concatenate([system] * (n // rank), 1), [rhs, basis_map], visit)
    weights = found[0]
    for part in found[1:]:
        weights = weights + part
    increment = dot(jnp.broadcast_to(weights, (8, n)), s_ref[...])
    for i in range(8):
        out_ref[i : i + 1, :] = mean_ref[i : i + 1, :] + increment[0:1, i * 128 : (i + 1) * 128]


def analysis(sums, mixers, s, mean):
    return pl.pallas_call(
        analysis_kernel,
        in_specs=[VMEM] * 6,
        out_specs=VMEM,
        out_shape=shape(8, 128),
        compiler_params=params(),
        cost_estimate=cost(16 << 20),
        name="analysis",
    )(sums, *mixers, s, mean)


def add_kernel(a_ref, b_ref, c_ref, d_ref, *rest):
    rest[-1][...] = (a_ref[...] + b_ref[...]) + (c_ref[...] + d_ref[...])


def add_up(a, b, c, d, *tokens):
    return pl.pallas_call(
        add_kernel,
        in_specs=[VMEM] * 4 + [ANY] * len(tokens),
        out_specs=VMEM,
        out_shape=shape(*a.shape),
        compiler_params=params(),
        cost_estimate=cost(1 << 18),
        name="add_up",
    )(a, b, c, d, *tokens)


def to_next(v):
    size = lax.axis_size("tile")
    return lax.ppermute(v, "tile", [(i, i + 1) for i in range(size - 1)])


def to_previous(v):
    size = lax.axis_size("tile")
    return lax.ppermute(v, "tile", [(i + 1, i) for i in range(size - 1)])


def across(v, axis, bits):
    return lax.ppermute(v, axis, [(i, i ^ bits) for i in range(lax.axis_size(axis))])


def local(prior, k, slots, merge, cells, values, var):
    members, levels, rows, width = prior.shape
    rank = merge.shape[2]
    groups = lax.axis_size("grp")
    tile, group = lax.axis_index("tile"), lax.axis_index("grp")
    chip, core = group // 2, group % 2
    place = jnp.stack([tile, group]).astype(jnp.int32)
    sums, low, high = pair_sums(prior, slots, k, rank)
    before = to_next(high)
    after = to_previous(low)
    kb, ka = before[3 * rank :], after[3 * rank :]

    lo, hi = pack(prior, 0, CHUNKS[0], low)
    arrived_a = to_next(hi), to_previous(lo)
    obs, *mixers = sensors(place, cells, values, var, merge, width // groups, lo)
    pieces = surface(sums, before, after, k, groups, obs)
    pieces = pieces.reshape(groups // 2, 2, rows, rank, width // groups)

    mine = lax.dynamic_index_in_dim(pieces, core, 1, False)
    other = lax.dynamic_index_in_dim(pieces, 1 - core, 1, False)
    pairs = jnp.stack([mine, across(other, "grp", 1)], 1)

    def pair_for(bits):
        return lax.dynamic_index_in_dim(pairs, chip ^ bits, 0, False)

    own = pair_for(0)
    r1, r3, r2 = (across(pair_for(bits), "grp", 2 * bits) for bits in (1, 3, 2))
    lo, hi = pack(prior, 8 * CHUNKS[0], CHUNKS[1], own)
    part, sketches, mean = gram(place, obs, own, r1, r2, r3, lo)
    lo, hi, part = lax.optimization_barrier((lo, hi, part))

    half = part.reshape(2, -1, part.shape[1])
    total = lax.dynamic_index_in_dim(half, core, 0, False) + across(
        lax.dynamic_index_in_dim(half, 1 - core, 0, False), "grp", 1
    )

    def others(v, axis, near):
        return [across(v, axis, near * bits) for bits in (1, 2, 3)]

    arrived_b = to_next(hi), to_previous(lo)
    parts = others(total, "grp", 2)
    out, done = two_steps(prior, *arrived_a, k, kb, ka, None, 0, part)
    total = add_up(total, *parts, done)
    total = add_up(total, *others(total, "tile", 4), *arrived_b)
    parts = others(total, "tile", 1)
    out, done = two_steps(prior, *arrived_b, k, kb, ka, out, 8 * CHUNKS[0], total)
    total = add_up(total, *parts, done)
    second = across(total, "grp", 1)
    both = jnp.where(core == 0, jnp.concatenate([total, second], 0), jnp.concatenate([second, total], 0))
    posterior = analysis(both, mixers, sketches, mean)
    return out, posterior


def solution(mesh):
    in_specs = (P("grp", None, "tile", None), P(None, "tile", None), P("grp"), P(), P(), P(), P())
    out_specs = (P("grp", None, "tile", None), P("tile", "grp"))
    return jax.shard_map(local, mesh=mesh, in_specs=in_specs, out_specs=out_specs, check_vma=False)
```

```python
import functools

import jax
import jax.numpy as jnp
from jax import lax
from jax.experimental import pallas as pl
from jax.experimental.pallas import tpu as pltpu
from jax.sharding import PartitionSpec as P

HI = lax.Precision.HIGHEST
VMEM = pl.BlockSpec(memory_space=pltpu.VMEM)
SMEM = pl.BlockSpec(memory_space=pltpu.SMEM)
ANY = pl.BlockSpec(memory_space=pl.ANY)
HBM = pl.BlockSpec(memory_space=pltpu.HBM)
ROWS = 8
LIMIT = 16 << 20
LARGE = 105 << 19
CHUNKS = (1, 2, 1)
F32 = jnp.float32


def shape(*dims):
    return jax.ShapeDtypeStruct(dims, F32)


def cost(nbytes, flops=0):
    return pl.CostEstimate(flops=flops, bytes_accessed=nbytes >> 10, transcendentals=0)


def params(limit=LIMIT):
    return pltpu.CompilerParams(vmem_limit_bytes=limit)


def lanes_sum(v):
    tiles = [v[:, t : t + 128] for t in range(0, v.shape[1], 128)]
    lane = lax.broadcasted_iota(jnp.int32, tiles[0].shape, 1)
    first, last = lane == 0, lane == 127
    ups = [jnp.zeros_like(tiles[0])] + [pltpu.roll(t, 1, 1) for t in tiles]
    downs = [pltpu.roll(t, 127, 1) for t in tiles] + [jnp.zeros_like(tiles[0])]
    out = [
        jnp.where(first, ups[t], ups[t + 1]) + jnp.where(last, downs[t + 1], downs[t])
        for t in range(len(tiles))
    ]
    return jnp.concatenate(out, 1)


def pair_kernel(slot_ref, k_ref, u_ref, sum_ref, low_ref, high_ref, pair_ref, seen_ref, order_ref, sem, k_sem):
    members, levels = u_ref.shape[:2]
    rank = sum_ref.shape[2]
    at = pl.ds(3 * rank, levels)
    turned = [
        pltpu.make_async_copy(k_ref.at[:, 0, :], low_ref.at[at], k_sem.at[0]),
        pltpu.make_async_copy(k_ref.at[:, ROWS - 1, :], high_ref.at[at], k_sem.at[1]),
    ]
    for copy in turned:
        copy.start()
    for s in range(rank):
        seen_ref[s] = 0

    def place(m, carry):
        s = slot_ref[m]
        which = jnp.minimum(seen_ref[s], 1)
        order_ref[2 * s + which] = m
        seen_ref[s] = which + 1
        return carry

    lax.fori_loop(0, members, place, 0)
    copies = [
        pltpu.make_async_copy(
            u_ref.at[order_ref[2 * s + i], pl.ds(levels - 3, 3)], pair_ref.at[i, :, :, s, :], sem.at[i, s]
        )
        for s in range(rank)
        for i in range(2)
    ]
    for copy in copies:
        copy.start()
    for copy in turned + copies:
        copy.wait()
    for l in range(3):
        for x in range(ROWS):
            sum_ref[l, x] = pair_ref[0, l, x] + pair_ref[1, l, x]
    for part, (level, x) in enumerate(((1, 0), (2, 0), (2, 1))):
        at = pl.ds(part * rank, rank)
        low_ref[at, :] = sum_ref[level, x]
        high_ref[at, :] = sum_ref[level, ROWS - 1 - x]


def pair_sums(prior, slots, k, rank):
    members, levels, rows, width = prior.shape
    edge = 3 * rank + levels
    return pl.pallas_call(
        pair_kernel,
        in_specs=[SMEM, HBM, HBM],
        out_specs=[VMEM] * 3,
        out_shape=[
            shape(3, rows, rank, width),
            shape(edge, width),
            shape(edge, width),
        ],
        scratch_shapes=[
            pltpu.VMEM((2, 3, rows, rank, width), F32),
            pltpu.SMEM((rank,), jnp.int32),
            pltpu.SMEM((members,), jnp.int32),
            pltpu.SemaphoreType.DMA((2, rank)),
            pltpu.SemaphoreType.DMA((2,)),
        ],
        compiler_params=params(54 << 20),
        cost_estimate=cost(6 << 20),
        name="pair_sums",
    )(slots, k, prior)


def pack_kernel(first, u_ref, *rest):
    low_ref, high_ref, sem = rest[-3:]
    groups, depth, _, span, _ = low_ref.shape
    copies = []
    for g in range(groups):
        for m in range(span):
            for r in range(depth):
                for side, (ref, x) in enumerate(((low_ref, r), (high_ref, ROWS - 1 - r))):
                    copies.append(
                        pltpu.make_async_copy(
                            u_ref.at[first + g * span + m, :, x, :], ref.at[g, r, :, m, :], sem.at[g, m, r, side]
                        )
                    )
    for copy in copies:
        copy.start()
    for copy in copies:
        copy.wait()


def pack(prior, first, groups, *tokens):
    levels, width = prior.shape[1], prior.shape[3]
    return pl.pallas_call(
        functools.partial(pack_kernel, first),
        in_specs=[HBM] + [ANY] * len(tokens),
        out_specs=[VMEM] * 2,
        out_shape=[shape(groups, 2, levels, 8, width)] * 2,
        scratch_shapes=[pltpu.SemaphoreType.DMA((groups, 8, 2, 2))],
        compiler_params=params(LARGE),
        cost_estimate=cost(groups << 21),
        name="pack_edges",
    )(prior, *tokens)


def step_kernel(first, u_ref, before_ref, after_ref, k_ref, kb_ref, ka_ref, *rest):
    out_ref, token_ref, u, v, w, in_sem, edge_sem, out_sem = rest[-8:]
    token_ref[...] = jnp.zeros_like(token_ref)
    levels, span, width = u_ref.shape[1], u.shape[3], u.shape[4]
    groups = before_ref.shape[0]
    skip = kb_ref.shape[0] - levels
    part = levels // 4

    def fetch(g, p):
        slot = g % 2
        at, to = pl.ds(p * part, part), pl.ds(p * part + 1, part)
        copies = [
            pltpu.make_async_copy(
                u_ref.at[first + g * span + m, at], u.at[slot, to, pl.ds(2, ROWS), m, :], in_sem.at[slot, p, m]
            )
            for m in range(span)
        ]
        for r in range(2):
            for side, (ref, x) in enumerate(((before_ref, 1 - r), (after_ref, ROWS + 2 + r))):
                copies.append(
                    pltpu.make_async_copy(ref.at[g, r, at], u.at[slot, to, x], edge_sem.at[slot, p, r, side])
                )
        return copies

    def store(g, p):
        slot, at = g % 2, pl.ds(p * part, part)
        return [
            pltpu.make_async_copy(
                w.at[slot, at, :, m, :], out_ref.at[first + g * span + m, at], out_sem.at[slot, p, m]
            )
            for m in range(span)
        ]

    parts = levels // part
    for p in range(parts):
        for copy in fetch(0, p):
            copy.start()
    zero = jnp.zeros((span, width), F32)
    for l in (0, levels + 1):
        for x in range(ROWS + 4):
            for slot in range(u.shape[0]):
                u[slot, l, x] = zero
        for x in range(ROWS + 2):
            v[l, x] = zero
    tile = (span, 128)
    lane = lax.broadcasted_iota(jnp.int32, tile, 1)
    left, right = lane == 0, lane == 127

    def tiles(ref, l, x):
        return [ref[l, x, :, t : t + 128] for t in range(0, width, 128)]

    def one_step(src, l, x, rows, k):
        blank = jnp.zeros(tile, F32)
        before, here, after = rows
        ups = [blank] + [pltpu.roll(h, 1, 1) for h in here]
        downs = [pltpu.roll(h, 127, 1) for h in here] + [blank]
        out = []
        for t, h in enumerate(here):
            cut = pl.ds(t * 128, 128)
            total = (before[t] + after[t]) + (src[l - 1, x, :, cut] + src[l + 1, x, :, cut])
            total += jnp.where(left, ups[t], ups[t + 1]) + jnp.where(right, downs[t + 1], downs[t])
            out.append(h + k[:, t * 128 : t * 128 + 128] * (total - 6.0 * h))
        return out

    for g in range(groups):
        slot = g % 2
        if g + 1 < groups:
            for p in range(parts):
                for copy in fetch(g + 1, p):
                    copy.start()
        if g >= 2:
            for p in range(parts):
                for copy in store(g - 2, p):
                    copy.wait()

        def first_step(l):
            rows = [tiles(u.at[slot], l + 1, x) for x in range(2)]
            for x in range(-1, ROWS + 1):
                rows = rows[-2:] + [tiles(u.at[slot], l + 1, x + 3)]
                if x < 0:
                    k = kb_ref[skip + l : skip + l + 1, :]
                elif x == ROWS:
                    k = ka_ref[skip + l : skip + l + 1, :]
                else:
                    k = k_ref[l, x : x + 1, :]
                for t, tile_out in enumerate(one_step(u.at[slot], l + 1, x + 2, rows, k)):
                    v[l + 1, x + 1, :, t * 128 : t * 128 + 128] = tile_out

        def second_step(l):
            rows = [tiles(v, l + 1, x) for x in range(2)]
            for x in range(ROWS):
                rows = rows[-2:] + [tiles(v, l + 1, x + 2)]
                for t, tile_out in enumerate(one_step(v, l + 1, x + 1, rows, k_ref[l, x : x + 1, :])):
                    w[slot, l, x, :, t * 128 : t * 128 + 128] = tile_out

        for copy in fetch(g, 0):
            copy.wait()
        first_step(0)
        done = 0
        for p in range(parts):
            if p + 1 < parts:
                for copy in fetch(g, p + 1):
                    copy.wait()
            top = (p + 1) * part if p + 1 < parts else levels - 1
            for l in range(done + 1, top + 1):
                first_step(l)
                second_step(l - 1)
            done = top
            if p + 1 < parts:
                for copy in store(g, p):
                    copy.start()
        second_step(levels - 1)
        for copy in store(g, parts - 1):
            copy.start()
    for g in range(max(groups - 2, 0), groups):
        for p in range(parts):
            for copy in store(g, p):
                copy.wait()


def two_steps(prior, before, after, k, kb, ka, done, first, *tokens):
    members, levels, rows, width = prior.shape
    slots = min(before.shape[0], 2)
    operands = [prior, before, after, k, kb, ka]
    specs = [HBM] + [ANY] * 2 + [VMEM] * 3
    aliases = {}
    if done is not None:
        operands.append(done)
        specs.append(HBM)
        aliases = {6: 0}
    return pl.pallas_call(
        functools.partial(step_kernel, first),
        in_specs=specs + [ANY] * len(tokens),
        out_specs=[HBM, VMEM],
        out_shape=[shape(*prior.shape), shape(8, 128)],
        scratch_shapes=[
            pltpu.VMEM((slots, levels + 2, rows + 4, 8, width), F32),
            pltpu.VMEM((levels + 2, rows + 2, 8, width), F32),
            pltpu.VMEM((slots, levels, rows, 8, width), F32),
            pltpu.SemaphoreType.DMA((slots, 4, 8)),
            pltpu.SemaphoreType.DMA((slots, 4, 2, 2)),
            pltpu.SemaphoreType.DMA((slots, 4, 8)),
        ],
        input_output_aliases=aliases,
        compiler_params=params(LARGE),
        cost_estimate=cost(before.shape[0] << 23),
        name="two_steps",
    )(*operands, *tokens)


def surface_kernel(p_ref, before_ref, after_ref, k_ref, *rest):
    out_ref = rest[-1]
    rank = p_ref.shape[2]
    top = before_ref.shape[0] - 1

    def edge(ref, x):
        low, near, far = (ref[i * rank : (i + 1) * rank, :] for i in range(3))
        k = ref[top : top + 1, :]
        return near + k * (low + far + p_ref[2, x] + lanes_sum(near) - 6.0 * near)

    v6, v7 = [], [edge(before_ref, 0)]
    for x in range(ROWS):
        u6, u7 = p_ref[1, x], p_ref[2, x]

        def beside(level, part):
            before = p_ref[level, x - 1] if x > 0 else before_ref[part * rank : (part + 1) * rank, :]
            after = p_ref[level, x + 1] if x < ROWS - 1 else after_ref[part * rank : (part + 1) * rank, :]
            return before + after

        v6.append(u6 + k_ref[0, x : x + 1, :] * (beside(1, 0) + lanes_sum(u6) + p_ref[0, x] + u7 - 6.0 * u6))
        v7.append(u7 + k_ref[1, x : x + 1, :] * (beside(2, 1) + lanes_sum(u7) + u6 - 6.0 * u7))
    v7.append(edge(after_ref, ROWS - 1))
    piece = out_ref.shape[3]
    for x in range(ROWS):
        here = v7[x + 1]
        total = v7[x] + v7[x + 2] + lanes_sum(here) + v6[x]
        out = here + k_ref[1, x : x + 1, :] * (total - 6.0 * here)
        for g in range(out_ref.shape[0]):
            out_ref[g, x] = out[:, g * piece : (g + 1) * piece]


def surface(sums, before, after, k, groups, *tokens):
    _, rows, rank, width = sums.shape
    levels = k.shape[0]
    edge = pl.BlockSpec(before.shape, lambda i: (0, 0))
    return pl.pallas_call(
        surface_kernel,
        grid=(1,),
        in_specs=[
            pl.BlockSpec(sums.shape, lambda i: (0, 0, 0, 0)),
            edge,
            edge,
            pl.BlockSpec((2, rows, width), lambda i: (levels // 2 - 1, 0, 0)),
        ]
        + [ANY] * len(tokens),
        out_specs=pl.BlockSpec((groups, rows, rank, width // groups), lambda i: (0, 0, 0, 0)),
        out_shape=shape(groups, rows, rank, width // groups),
        compiler_params=params(),
        cost_estimate=cost(4 << 20),
        name="surface_steps",
    )(sums, before, after, k, *tokens)


def sensor_kernel(at_ref, cell_ref, value_ref, var_ref, m_ref, *rest):
    rank = m_ref.shape[2]
    out_ref, *mix_refs = rest[-1 - m_ref.shape[0] :]
    for level, ref in enumerate(mix_refs):
        ref[...] = jnp.zeros_like(ref)
        turned = m_ref[level].T
        for p in range(ref.shape[0] // rank):
            ref[p * rank : (p + 1) * rank, 2 * p * rank : 2 * (p + 1) * rank] = turned
    width, columns = 1024, out_ref.shape[1]
    rows = out_ref.shape[0] // 2
    chunks, span = cell_ref.shape
    weight = 1.0 / var_ref[...]
    local = cell_ref[...] - at_ref[0] * (rows * width)
    x = local // width
    y = local - x * width - at_ref[1] * columns
    left, right = [], []
    row = lax.broadcasted_iota(jnp.int32, (rows, span), 0)
    column = lax.broadcasted_iota(jnp.int32, (columns, span), 0)
    weighted = weight * value_ref[...]
    for c in range(chunks):
        hit = x[c : c + 1, :] == row
        left.append(
            jnp.concatenate(
                [jnp.where(hit, weight[c : c + 1, :], 0.0), jnp.where(hit, weighted[c : c + 1, :], 0.0)], 0
            )
        )
        right.append(jnp.where(y[c : c + 1, :] == column, 1.0, 0.0))
    out_ref[...] = lax.dot_general(
        jnp.concatenate(left, 1),
        jnp.concatenate(right, 1),
        (((1,), (1,)), ((), ())),
        precision=HI,
        preferred_element_type=F32,
    )


def sensors(place, cells, values, var, merge, columns, *tokens):
    rank = merge.shape[2]
    mixers = [shape(rank << i, 2 * rank << i) for i in range(merge.shape[0])][::-1]
    return pl.pallas_call(
        sensor_kernel,
        in_specs=[SMEM] + [VMEM] * 4 + [ANY] * len(tokens),
        out_specs=[VMEM] * (1 + len(mixers)),
        out_shape=[shape(16, columns)] + mixers,
        compiler_params=params(),
        cost_estimate=cost(4 << 20),
        name="sensor_sums",
    )(place, *(a.reshape(-1, 128) for a in (cells, values, var)), merge, *tokens)


def gram_kernel(place_ref, obs_ref, own_ref, r1_ref, r2_ref, r3_ref, *rest):
    sums_ref, s_ref, mean_ref, raw_ref = rest[-4:]
    chip, core = place_ref[1] // 2, place_ref[1] % 2
    for d, ref in ((0, own_ref), (1, r1_ref), (2, r2_ref), (3, r3_ref)):
        for slot in range(2):
            group = jnp.bitwise_xor(chip, d) * 2 + jnp.bitwise_xor(core, slot)
            rank = ref.shape[2]
            at = pl.ds(pl.multiple_of(group * rank, rank), rank)
            for x in range(ROWS):
                raw_ref[x, at, :] = ref[slot, x]
    total = None
    sketches = raw_ref.shape[1]
    member_total = 2 * sketches
    for x in range(0, 8, 2):
        both, means, weights, values = [], [], [], []
        for i in (x, x + 1):
            raw = raw_ref[i]
            mean = jnp.sum(raw, axis=0, keepdims=True) * (1.0 / member_total)
            dev = raw - 2.0 * mean
            s_ref[:, i * 128 : (i + 1) * 128] = dev
            mean_ref[i : i + 1, :] = mean
            both.append(dev)
            w = obs_ref[i : i + 1, :]
            weights.append(w)
            values.append(obs_ref[8 + i : 9 + i, :] - mean * w)
        dev = jnp.concatenate(both, 1)
        w = jnp.concatenate(weights, 1)
        z = jnp.broadcast_to(jnp.concatenate(values, 1), (8, dev.shape[1]))
        left = jnp.concatenate([dev, dev * w, z], 0)
        part = lax.dot_general(left, dev, (((1,), (1,)), ((), ())), precision=HI, preferred_element_type=F32)
        total = part if total is None else total + part
    gram, weighted, rhs = total[:sketches], total[sketches : 2 * sketches], total[2 * sketches :]
    row = lax.broadcasted_iota(jnp.int32, gram.shape, 0)
    lane = lax.broadcasted_iota(jnp.int32, gram.shape, 1)
    sums_ref[0:sketches, :] = jnp.where(lane > row, gram, weighted)
    sums_ref[sketches : sketches + 8, :] = jnp.broadcast_to(
        jnp.sum(jnp.where(lane == row, gram, 0.0), axis=0, keepdims=True), (8, 128)
    )
    sums_ref[sketches + 8 : sketches + 16, :] = rhs


def gram(place, obs, own, r1, r2, r3, *tokens):
    return pl.pallas_call(
        gram_kernel,
        in_specs=[SMEM] + [VMEM] * 5 + [ANY] * len(tokens),
        out_specs=[VMEM] * 3,
        out_shape=[shape(144, 128), shape(128, 1024), shape(8, 128)],
        scratch_shapes=[pltpu.VMEM((8, 128, 128), F32)],
        compiler_params=params(),
        cost_estimate=cost(4 << 20),
        name="gram_sums",
    )(place, obs, own, r1, r2, r3, *tokens)


def dot(a, b, ca=1, cb=0):
    return lax.dot_general(a, b, (((ca,), (cb,)), ((), ())), precision=HI, preferred_element_type=F32)


def analysis_kernel(sums_ref, mix0_ref, mix1_ref, mix2_ref, s_ref, mean_ref, out_ref):
    n = 128
    mixers = (mix0_ref, mix1_ref, mix2_ref)
    rank = mix2_ref.shape[0]
    packed = sums_ref[0:n, :]
    row = lax.broadcasted_iota(jnp.int32, (n, n), 0)
    lane = lax.broadcasted_iota(jnp.int32, (n, n), 1)
    upper = jnp.where(lane > row, packed, 0.0)
    lower = jnp.where(lane < row, packed, 0.0)
    g = upper + upper.T + jnp.where(lane == row, sums_ref[n : n + 1, :], 0.0)
    h = lower + lower.T + jnp.where(lane == row, packed, 0.0)
    q = sums_ref[n + 8 : n + 9, :]

    block = (rank, n)
    sub = lax.broadcasted_iota(jnp.int32, block, 0)
    at = lax.broadcasted_iota(jnp.int32, block, 1)
    unit = jnp.where(at % rank == sub, 1.0, 0.0)

    def eliminate(d, extra, visit=None):
        columns = [jnp.take_along_axis(d, at // rank * rank + j, axis=1) for j in range(rank)]
        for j in range(rank):
            c = columns[j]
            inverse = 1.0 / c[j : j + 1, :]
            if visit is not None:
                visit(j, inverse, extra)
            if j == rank - 1:
                break
            factor = jnp.where(sub > j, c * inverse, 0.0)
            for k in range(j + 1, rank):
                columns[k] = columns[k] - factor * c[k : k + 1, :]
            extra = [e - factor * e[j : j + 1, :] for e in extra]
        return extra

    def widened(v):
        if v.shape[1] == n:
            return v
        return jnp.concatenate([v, jnp.zeros((rank, n - v.shape[1]), F32)], 1) + jnp.where(
            at >= v.shape[1], unit, 0.0
        )

    c = g
    w = None
    for mix_ref in mixers:
        size = c.shape[0]
        d = jnp.zeros((rank, size), F32)
        for b in range(size // rank):
            d = d + jnp.where(at[:, :size] // rank == b, c[b * rank : (b + 1) * rank, :], 0.0)
        (t,) = eliminate(widened(d), [unit])
        t = jnp.concatenate([t[:, :size]] * (size // rank), 0)
        t = jnp.where(row[:size, :size] // rank == lane[:size, :size] // rank, t, 0.0)
        x = dot(mix_ref[...], t)
        c = dot(dot(x, c), x, 1, 1)
        w = x if w is None else dot(x, w)
    h3 = dot(dot(w, h), w, 1, 1)
    (t3,) = eliminate(widened(c), [unit])
    t3 = t3[:, :rank]
    basis_map = dot(t3, w)
    eye = unit[:, :rank]
    system = 255.0 * eye + dot(dot(t3, h3), t3, 1, 1)
    rhs = jnp.broadcast_to(jnp.sum(basis_map * q, axis=1, keepdims=True), block)
    found = []

    def visit(j, inverse, extra):
        y, v = extra
        found.append((y[j : j + 1, :] * inverse[:, 0:1]) * v[j : j + 1, :])

    eliminate(jnp.concatenate([system] * (n // rank), 1), [rhs, basis_map], visit)
    weights = found[0]
    for part in found[1:]:
        weights = weights + part
    increment = dot(jnp.broadcast_to(weights, (8, n)), s_ref[...])
    for i in range(8):
        out_ref[i : i + 1, :] = mean_ref[i : i + 1, :] + increment[0:1, i * 128 : (i + 1) * 128]


def analysis(sums, mixers, s, mean):
    return pl.pallas_call(
        analysis_kernel,
        in_specs=[VMEM] * 6,
        out_specs=VMEM,
        out_shape=shape(8, 128),
        compiler_params=params(),
        cost_estimate=cost(16 << 20),
        name="analysis",
    )(sums, *mixers, s, mean)


def add_kernel(a_ref, b_ref, c_ref, d_ref, *rest):
    rest[-1][...] = (a_ref[...] + b_ref[...]) + (c_ref[...] + d_ref[...])


def add_up(a, b, c, d, *tokens):
    return pl.pallas_call(
        add_kernel,
        in_specs=[VMEM] * 4 + [ANY] * len(tokens),
        out_specs=VMEM,
        out_shape=shape(*a.shape),
        compiler_params=params(),
        cost_estimate=cost(1 << 18),
        name="add_up",
    )(a, b, c, d, *tokens)


def to_next(v):
    size = lax.axis_size("tile")
    return lax.ppermute(v, "tile", [(i, i + 1) for i in range(size - 1)])


def to_previous(v):
    size = lax.axis_size("tile")
    return lax.ppermute(v, "tile", [(i + 1, i) for i in range(size - 1)])


def across(v, axis, bits):
    return lax.ppermute(v, axis, [(i, i ^ bits) for i in range(lax.axis_size(axis))])


def local(prior, k, slots, merge, cells, values, var):
    members, levels, rows, width = prior.shape
    rank = merge.shape[2]
    groups = lax.axis_size("grp")
    tile, group = lax.axis_index("tile"), lax.axis_index("grp")
    chip, core = group // 2, group % 2
    place = jnp.stack([tile, group]).astype(jnp.int32)
    sums, low, high = pair_sums(prior, slots, k, rank)
    before = to_next(high)
    after = to_previous(low)

    lo, hi = pack(prior, 0, CHUNKS[0], low)
    arrived_a = to_next(hi), to_previous(lo)
    obs, *mixers = sensors(place, cells, values, var, merge, width // groups, lo)
    pieces = surface(sums, before, after, k, groups, obs)
    pieces = pieces.reshape(groups // 2, 2, rows, rank, width // groups)

    mine = lax.dynamic_index_in_dim(pieces, core, 1, False)
    other = lax.dynamic_index_in_dim(pieces, 1 - core, 1, False)
    pairs = jnp.stack([mine, across(other, "grp", 1)], 1)

    def pair_for(bits):
        return lax.dynamic_index_in_dim(pairs, chip ^ bits, 0, False)

    own = pair_for(0)
    r1, r3, r2 = (across(pair_for(bits), "grp", 2 * bits) for bits in (1, 3, 2))
    lo, hi = pack(prior, 8 * CHUNKS[0], CHUNKS[1], own)
    r1, r2, r3, *arrived_a = lax.optimization_barrier((r1, r2, r3, *arrived_a))
    part, sketches, mean = gram(place, obs, own, r1, r2, r3, lo)
    lo, hi, part = lax.optimization_barrier((lo, hi, part))

    half = part.reshape(2, -1, part.shape[1])
    total = lax.dynamic_index_in_dim(half, core, 0, False) + across(
        lax.dynamic_index_in_dim(half, 1 - core, 0, False), "grp", 1
    )

    def others(v, axis, near):
        return [across(v, axis, near * bits) for bits in (1, 2, 3)]

    arrived_b = to_next(hi), to_previous(lo)
    parts = others(total, "grp", 2)
    lo, hi = pack(prior, 8 * sum(CHUNKS[:2]), CHUNKS[2], part)
    out, done = two_steps(prior, *arrived_a, k, before, after, None, 0, lo)
    total = add_up(total, *parts, done)
    lo, hi, total = lax.optimization_barrier((lo, hi, total))
    arrived_c = to_next(hi), to_previous(lo)
    out, done = two_steps(prior, *arrived_b, k, before, after, out, 8 * CHUNKS[0], total)
    total, done = lax.optimization_barrier((total, done))
    total = add_up(total, *others(total, "tile", 4))
    total, *arrived_c = lax.optimization_barrier((total, *arrived_c))
    parts = others(total, "tile", 1)
    out, done = two_steps(prior, *arrived_c, k, before, after, out, 8 * sum(CHUNKS[:2]), total)
    total = add_up(total, *parts, done)
    second = across(total, "grp", 1)
    both = jnp.where(core == 0, jnp.concatenate([total, second], 0), jnp.concatenate([second, total], 0))
    posterior = analysis(both, mixers, sketches, mean)
    return out, posterior


def solution(mesh):
    in_specs = (P("grp", None, "tile", None), P(None, "tile", None), P("grp"), P(), P(), P(), P())
    out_specs = (P("grp", None, "tile", None), P("tile", "grp"))
    return jax.shard_map(local, mesh=mesh, in_specs=in_specs, out_specs=out_specs, check_vma=False)
```

```python
import functools

import jax
import jax.numpy as jnp
from jax import lax
from jax.experimental import pallas as pl
from jax.experimental.pallas import tpu as pltpu
from jax.sharding import PartitionSpec as P

HI = lax.Precision.HIGHEST
VMEM = pl.BlockSpec(memory_space=pltpu.VMEM)
SMEM = pl.BlockSpec(memory_space=pltpu.SMEM)
ANY = pl.BlockSpec(memory_space=pl.ANY)
HBM = pl.BlockSpec(memory_space=pltpu.HBM)
ROWS = 8
LIMIT = 16 << 20
LARGE = 105 << 19
CHUNKS = (1, 2, 1)
F32 = jnp.float32


def shape(*dims):
    return jax.ShapeDtypeStruct(dims, F32)


def cost(nbytes, flops=0):
    return pl.CostEstimate(flops=flops, bytes_accessed=nbytes >> 10, transcendentals=0)


def params(limit=LIMIT):
    return pltpu.CompilerParams(vmem_limit_bytes=limit)


def lanes_sum(v):
    tiles = [v[:, t : t + 128] for t in range(0, v.shape[1], 128)]
    lane = lax.broadcasted_iota(jnp.int32, tiles[0].shape, 1)
    first, last = lane == 0, lane == 127
    ups = [jnp.zeros_like(tiles[0])] + [pltpu.roll(t, 1, 1) for t in tiles]
    downs = [pltpu.roll(t, 127, 1) for t in tiles] + [jnp.zeros_like(tiles[0])]
    out = [
        jnp.where(first, ups[t], ups[t + 1]) + jnp.where(last, downs[t + 1], downs[t])
        for t in range(len(tiles))
    ]
    return jnp.concatenate(out, 1)


def pair_kernel(slot_ref, k_ref, u_ref, sum_ref, low_ref, high_ref, pair_ref, seen_ref, order_ref, sem, k_sem):
    members, levels = u_ref.shape[:2]
    rank = sum_ref.shape[2]
    at = pl.ds(3 * rank, levels)
    turned = [
        pltpu.make_async_copy(k_ref.at[:, 0, :], low_ref.at[at], k_sem.at[0]),
        pltpu.make_async_copy(k_ref.at[:, ROWS - 1, :], high_ref.at[at], k_sem.at[1]),
    ]
    for copy in turned:
        copy.start()
    for s in range(rank):
        seen_ref[s] = 0

    def place(m, carry):
        s = slot_ref[m]
        which = jnp.minimum(seen_ref[s], 1)
        order_ref[2 * s + which] = m
        seen_ref[s] = which + 1
        return carry

    lax.fori_loop(0, members, place, 0)
    copies = [
        pltpu.make_async_copy(
            u_ref.at[order_ref[2 * s + i], pl.ds(levels - 3, 3)], pair_ref.at[i, :, :, s, :], sem.at[i, s]
        )
        for s in range(rank)
        for i in range(2)
    ]
    for copy in copies:
        copy.start()
    for copy in turned + copies:
        copy.wait()
    for l in range(3):
        for x in range(ROWS):
            sum_ref[l, x] = pair_ref[0, l, x] + pair_ref[1, l, x]
    for part, (level, x) in enumerate(((1, 0), (2, 0), (2, 1))):
        at = pl.ds(part * rank, rank)
        low_ref[at, :] = sum_ref[level, x]
        high_ref[at, :] = sum_ref[level, ROWS - 1 - x]


def pair_sums(prior, slots, k, rank):
    members, levels, rows, width = prior.shape
    edge = 3 * rank + levels
    return pl.pallas_call(
        pair_kernel,
        in_specs=[SMEM, HBM, HBM],
        out_specs=[VMEM] * 3,
        out_shape=[
            shape(3, rows, rank, width),
            shape(edge, width),
            shape(edge, width),
        ],
        scratch_shapes=[
            pltpu.VMEM((2, 3, rows, rank, width), F32),
            pltpu.SMEM((rank,), jnp.int32),
            pltpu.SMEM((members,), jnp.int32),
            pltpu.SemaphoreType.DMA((2, rank)),
            pltpu.SemaphoreType.DMA((2,)),
        ],
        compiler_params=params(54 << 20),
        cost_estimate=cost(6 << 20),
        name="pair_sums",
    )(slots, k, prior)


def pack_kernel(first, u_ref, *rest):
    low_ref, high_ref, sem = rest[-3:]
    groups, depth, _, span, _ = low_ref.shape
    copies = []
    for g in range(groups):
        for m in range(span):
            for r in range(depth):
                for side, (ref, x) in enumerate(((low_ref, r), (high_ref, ROWS - 1 - r))):
                    copies.append(
                        pltpu.make_async_copy(
                            u_ref.at[first + g * span + m, :, x, :], ref.at[g, r, :, m, :], sem.at[g, m, r, side]
                        )
                    )
    for copy in copies:
        copy.start()
    for copy in copies:
        copy.wait()


def pack(prior, first, groups, *tokens):
    levels, width = prior.shape[1], prior.shape[3]
    return pl.pallas_call(
        functools.partial(pack_kernel, first),
        in_specs=[HBM] + [ANY] * len(tokens),
        out_specs=[VMEM] * 2,
        out_shape=[shape(groups, 2, levels, 8, width)] * 2,
        scratch_shapes=[pltpu.SemaphoreType.DMA((groups, 8, 2, 2))],
        compiler_params=params(LARGE),
        cost_estimate=cost(groups << 21),
        name="pack_edges",
    )(prior, *tokens)


def step_kernel(first, u_ref, before_ref, after_ref, k_ref, kb_ref, ka_ref, *rest):
    out_ref, token_ref, u, v, w, in_sem, edge_sem, out_sem = rest[-8:]
    token_ref[...] = jnp.zeros_like(token_ref)
    levels, span, width = u_ref.shape[1], u.shape[3], u.shape[4]
    groups = before_ref.shape[0]
    skip = kb_ref.shape[0] - levels
    part = levels // 4

    def fetch(g, p):
        slot = g % 2
        at, to = pl.ds(p * part, part), pl.ds(p * part + 1, part)
        copies = [
            pltpu.make_async_copy(
                u_ref.at[first + g * span + m, at], u.at[slot, to, pl.ds(2, ROWS), m, :], in_sem.at[slot, p, m]
            )
            for m in range(span)
        ]
        for r in range(2):
            for side, (ref, x) in enumerate(((before_ref, 1 - r), (after_ref, ROWS + 2 + r))):
                copies.append(
                    pltpu.make_async_copy(ref.at[g, r, at], u.at[slot, to, x], edge_sem.at[slot, p, r, side])
                )
        return copies

    def store(g, p):
        slot, at = g % 2, pl.ds(p * part, part)
        return [
            pltpu.make_async_copy(
                w.at[slot, at, :, m, :], out_ref.at[first + g * span + m, at], out_sem.at[slot, p, m]
            )
            for m in range(span)
        ]

    parts = levels // part
    for p in range(parts):
        for copy in fetch(0, p):
            copy.start()
    zero = jnp.zeros((span, width), F32)
    for l in (0, levels + 1):
        for x in range(ROWS + 4):
            for slot in range(u.shape[0]):
                u[slot, l, x] = zero
        for x in range(ROWS + 2):
            v[l, x] = zero
    tile = (span, 128)
    lane = lax.broadcasted_iota(jnp.int32, tile, 1)
    left, right = lane == 0, lane == 127

    def tiles(ref, l, x):
        return [ref[l, x, :, t : t + 128] for t in range(0, width, 128)]

    def one_step(src, l, x, rows, k):
        blank = jnp.zeros(tile, F32)
        before, here, after = rows
        ups = [blank] + [pltpu.roll(h, 1, 1) for h in here]
        downs = [pltpu.roll(h, 127, 1) for h in here] + [blank]
        out = []
        for t, h in enumerate(here):
            cut = pl.ds(t * 128, 128)
            total = (before[t] + after[t]) + (src[l - 1, x, :, cut] + src[l + 1, x, :, cut])
            total += jnp.where(left, ups[t], ups[t + 1]) + jnp.where(right, downs[t + 1], downs[t])
            out.append(h + k[:, t * 128 : t * 128 + 128] * (total - 6.0 * h))
        return out

    for g in range(groups):
        slot = g % 2
        if g + 1 < groups:
            for p in range(parts):
                for copy in fetch(g + 1, p):
                    copy.start()
        if g >= 2:
            for p in range(parts):
                for copy in store(g - 2, p):
                    copy.wait()

        def first_step(l):
            rows = [tiles(u.at[slot], l + 1, x) for x in range(2)]
            for x in range(-1, ROWS + 1):
                rows = rows[-2:] + [tiles(u.at[slot], l + 1, x + 3)]
                if x < 0:
                    k = kb_ref[skip + l : skip + l + 1, :]
                elif x == ROWS:
                    k = ka_ref[skip + l : skip + l + 1, :]
                else:
                    k = k_ref[l, x : x + 1, :]
                for t, tile_out in enumerate(one_step(u.at[slot], l + 1, x + 2, rows, k)):
                    v[l + 1, x + 1, :, t * 128 : t * 128 + 128] = tile_out

        def second_step(l):
            rows = [tiles(v, l + 1, x) for x in range(2)]
            for x in range(ROWS):
                rows = rows[-2:] + [tiles(v, l + 1, x + 2)]
                for t, tile_out in enumerate(one_step(v, l + 1, x + 1, rows, k_ref[l, x : x + 1, :])):
                    w[slot, l, x, :, t * 128 : t * 128 + 128] = tile_out

        for copy in fetch(g, 0):
            copy.wait()
        first_step(0)
        done = 0
        for p in range(parts):
            if p + 1 < parts:
                for copy in fetch(g, p + 1):
                    copy.wait()
            top = (p + 1) * part if p + 1 < parts else levels - 1
            for l in range(done + 1, top + 1):
                first_step(l)
                second_step(l - 1)
            done = top
            if p + 1 < parts:
                for copy in store(g, p):
                    copy.start()
        second_step(levels - 1)
        for copy in store(g, parts - 1):
            copy.start()
    for g in range(max(groups - 2, 0), groups):
        for p in range(parts):
            for copy in store(g, p):
                copy.wait()


def two_steps(prior, before, after, k, kb, ka, done, first, *tokens):
    members, levels, rows, width = prior.shape
    slots = min(before.shape[0], 2)
    operands = [prior, before, after, k, kb, ka]
    specs = [HBM] + [ANY] * 2 + [VMEM] * 3
    aliases = {}
    if done is not None:
        operands.append(done)
        specs.append(HBM)
        aliases = {6: 0}
    return pl.pallas_call(
        functools.partial(step_kernel, first),
        in_specs=specs + [ANY] * len(tokens),
        out_specs=[HBM, VMEM],
        out_shape=[shape(*prior.shape), shape(8, 128)],
        scratch_shapes=[
            pltpu.VMEM((slots, levels + 2, rows + 4, 8, width), F32),
            pltpu.VMEM((levels + 2, rows + 2, 8, width), F32),
            pltpu.VMEM((slots, levels, rows, 8, width), F32),
            pltpu.SemaphoreType.DMA((slots, 4, 8)),
            pltpu.SemaphoreType.DMA((slots, 4, 2, 2)),
            pltpu.SemaphoreType.DMA((slots, 4, 8)),
        ],
        input_output_aliases=aliases,
        compiler_params=params(LARGE),
        cost_estimate=cost(before.shape[0] << 23),
        name="two_steps",
    )(*operands, *tokens)


def surface_kernel(p_ref, before_ref, after_ref, k_ref, *rest):
    out_ref = rest[-1]
    rank = p_ref.shape[2]
    top = before_ref.shape[0] - 1

    def edge(ref, x):
        low, near, far = (ref[i * rank : (i + 1) * rank, :] for i in range(3))
        k = ref[top : top + 1, :]
        return near + k * (low + far + p_ref[2, x] + lanes_sum(near) - 6.0 * near)

    v6, v7 = [], [edge(before_ref, 0)]
    for x in range(ROWS):
        u6, u7 = p_ref[1, x], p_ref[2, x]

        def beside(level, part):
            before = p_ref[level, x - 1] if x > 0 else before_ref[part * rank : (part + 1) * rank, :]
            after = p_ref[level, x + 1] if x < ROWS - 1 else after_ref[part * rank : (part + 1) * rank, :]
            return before + after

        v6.append(u6 + k_ref[0, x : x + 1, :] * (beside(1, 0) + lanes_sum(u6) + p_ref[0, x] + u7 - 6.0 * u6))
        v7.append(u7 + k_ref[1, x : x + 1, :] * (beside(2, 1) + lanes_sum(u7) + u6 - 6.0 * u7))
    v7.append(edge(after_ref, ROWS - 1))
    piece = out_ref.shape[3]
    for x in range(ROWS):
        here = v7[x + 1]
        total = v7[x] + v7[x + 2] + lanes_sum(here) + v6[x]
        out = here + k_ref[1, x : x + 1, :] * (total - 6.0 * here)
        for g in range(out_ref.shape[0]):
            out_ref[g, x] = out[:, g * piece : (g + 1) * piece]


def surface(sums, before, after, k, groups, *tokens):
    _, rows, rank, width = sums.shape
    levels = k.shape[0]
    edge = pl.BlockSpec(before.shape, lambda i: (0, 0))
    return pl.pallas_call(
        surface_kernel,
        grid=(1,),
        in_specs=[
            pl.BlockSpec(sums.shape, lambda i: (0, 0, 0, 0)),
            edge,
            edge,
            pl.BlockSpec((2, rows, width), lambda i: (levels // 2 - 1, 0, 0)),
        ]
        + [ANY] * len(tokens),
        out_specs=pl.BlockSpec((groups, rows, rank, width // groups), lambda i: (0, 0, 0, 0)),
        out_shape=shape(groups, rows, rank, width // groups),
        compiler_params=params(),
        cost_estimate=cost(4 << 20),
        name="surface_steps",
    )(sums, before, after, k, *tokens)


def sensor_kernel(at_ref, cell_ref, value_ref, var_ref, m_ref, *rest):
    rank = m_ref.shape[2]
    out_ref, *mix_refs = rest[-1 - m_ref.shape[0] :]
    for level, ref in enumerate(mix_refs):
        ref[...] = jnp.zeros_like(ref)
        turned = m_ref[level].T
        for p in range(ref.shape[0] // rank):
            ref[p * rank : (p + 1) * rank, 2 * p * rank : 2 * (p + 1) * rank] = turned
    width, columns = 1024, out_ref.shape[1]
    rows = out_ref.shape[0] // 2
    chunks, span = cell_ref.shape
    weight = 1.0 / var_ref[...]
    local = cell_ref[...] - at_ref[0] * (rows * width)
    x = local // width
    y = local - x * width - at_ref[1] * columns
    left, right = [], []
    row = lax.broadcasted_iota(jnp.int32, (rows, span), 0)
    column = lax.broadcasted_iota(jnp.int32, (columns, span), 0)
    weighted = weight * value_ref[...]
    for c in range(chunks):
        hit = x[c : c + 1, :] == row
        left.append(
            jnp.concatenate(
                [jnp.where(hit, weight[c : c + 1, :], 0.0), jnp.where(hit, weighted[c : c + 1, :], 0.0)], 0
            )
        )
        right.append(jnp.where(y[c : c + 1, :] == column, 1.0, 0.0))
    out_ref[...] = lax.dot_general(
        jnp.concatenate(left, 1),
        jnp.concatenate(right, 1),
        (((1,), (1,)), ((), ())),
        precision=HI,
        preferred_element_type=F32,
    )


def sensors(place, cells, values, var, merge, columns, *tokens):
    rank = merge.shape[2]
    mixers = [shape(rank << i, 2 * rank << i) for i in range(merge.shape[0])][::-1]
    return pl.pallas_call(
        sensor_kernel,
        in_specs=[SMEM] + [VMEM] * 4 + [ANY] * len(tokens),
        out_specs=[VMEM] * (1 + len(mixers)),
        out_shape=[shape(16, columns)] + mixers,
        compiler_params=params(),
        cost_estimate=cost(4 << 20),
        name="sensor_sums",
    )(place, *(a.reshape(-1, 128) for a in (cells, values, var)), merge, *tokens)


def gram_kernel(place_ref, obs_ref, own_ref, r1_ref, r2_ref, r3_ref, *rest):
    sums_ref, s_ref, mean_ref, raw_ref = rest[-4:]
    chip, core = place_ref[1] // 2, place_ref[1] % 2
    for d, ref in ((0, own_ref), (1, r1_ref), (2, r2_ref), (3, r3_ref)):
        for slot in range(2):
            group = jnp.bitwise_xor(chip, d) * 2 + jnp.bitwise_xor(core, slot)
            rank = ref.shape[2]
            at = pl.ds(pl.multiple_of(group * rank, rank), rank)
            for x in range(ROWS):
                raw_ref[x, at, :] = ref[slot, x]
    total = None
    sketches = raw_ref.shape[1]
    member_total = 2 * sketches
    for x in range(0, 8, 2):
        both, means, weights, values = [], [], [], []
        for i in (x, x + 1):
            raw = raw_ref[i]
            mean = jnp.sum(raw, axis=0, keepdims=True) * (1.0 / member_total)
            dev = raw - 2.0 * mean
            s_ref[:, i * 128 : (i + 1) * 128] = dev
            mean_ref[i : i + 1, :] = mean
            both.append(dev)
            w = obs_ref[i : i + 1, :]
            weights.append(w)
            values.append(obs_ref[8 + i : 9 + i, :] - mean * w)
        dev = jnp.concatenate(both, 1)
        w = jnp.concatenate(weights, 1)
        z = jnp.broadcast_to(jnp.concatenate(values, 1), (8, dev.shape[1]))
        left = jnp.concatenate([dev, dev * w, z], 0)
        part = lax.dot_general(left, dev, (((1,), (1,)), ((), ())), precision=HI, preferred_element_type=F32)
        total = part if total is None else total + part
    gram, weighted, rhs = total[:sketches], total[sketches : 2 * sketches], total[2 * sketches :]
    row = lax.broadcasted_iota(jnp.int32, gram.shape, 0)
    lane = lax.broadcasted_iota(jnp.int32, gram.shape, 1)
    sums_ref[0:sketches, :] = jnp.where(lane > row, gram, weighted)
    sums_ref[sketches : sketches + 8, :] = jnp.broadcast_to(
        jnp.sum(jnp.where(lane == row, gram, 0.0), axis=0, keepdims=True), (8, 128)
    )
    sums_ref[sketches + 8 : sketches + 16, :] = rhs


def gram(place, obs, own, r1, r2, r3, *tokens):
    return pl.pallas_call(
        gram_kernel,
        in_specs=[SMEM] + [VMEM] * 5 + [ANY] * len(tokens),
        out_specs=[VMEM] * 3,
        out_shape=[shape(144, 128), shape(128, 1024), shape(8, 128)],
        scratch_shapes=[pltpu.VMEM((8, 128, 128), F32)],
        compiler_params=params(),
        cost_estimate=cost(4 << 20),
        name="gram_sums",
    )(place, obs, own, r1, r2, r3, *tokens)


def dot(a, b, ca=1, cb=0):
    return lax.dot_general(a, b, (((ca,), (cb,)), ((), ())), precision=HI, preferred_element_type=F32)


def analysis_kernel(sums_ref, mix0_ref, mix1_ref, mix2_ref, s_ref, mean_ref, out_ref):
    n = 128
    mixers = (mix0_ref, mix1_ref, mix2_ref)
    rank = mix2_ref.shape[0]
    packed = sums_ref[0:n, :]
    row = lax.broadcasted_iota(jnp.int32, (n, n), 0)
    lane = lax.broadcasted_iota(jnp.int32, (n, n), 1)
    upper = jnp.where(lane > row, packed, 0.0)
    lower = jnp.where(lane < row, packed, 0.0)
    g = upper + upper.T + jnp.where(lane == row, sums_ref[n : n + 1, :], 0.0)
    h = lower + lower.T + jnp.where(lane == row, packed, 0.0)
    q = sums_ref[n + 8 : n + 9, :]

    block = (rank, n)
    sub = lax.broadcasted_iota(jnp.int32, block, 0)
    at = lax.broadcasted_iota(jnp.int32, block, 1)
    unit = jnp.where(at % rank == sub, 1.0, 0.0)

    def eliminate(d, extra, visit=None):
        columns = [jnp.take_along_axis(d, at // rank * rank + j, axis=1) for j in range(rank)]
        for j in range(rank):
            c = columns[j]
            inverse = 1.0 / c[j : j + 1, :]
            if visit is not None:
                visit(j, inverse, extra)
            if j == rank - 1:
                break
            factor = jnp.where(sub > j, c * inverse, 0.0)
            for k in range(j + 1, rank):
                columns[k] = columns[k] - factor * c[k : k + 1, :]
            extra = [e - factor * e[j : j + 1, :] for e in extra]
        return extra

    def widened(v):
        if v.shape[1] == n:
            return v
        return jnp.concatenate([v, jnp.zeros((rank, n - v.shape[1]), F32)], 1) + jnp.where(
            at >= v.shape[1], unit, 0.0
        )

    c = g
    w = None
    for mix_ref in mixers:
        size = c.shape[0]
        d = jnp.zeros((rank, size), F32)
        for b in range(size // rank):
            d = d + jnp.where(at[:, :size] // rank == b, c[b * rank : (b + 1) * rank, :], 0.0)
        (t,) = eliminate(widened(d), [unit])
        t = jnp.concatenate([t[:, :size]] * (size // rank), 0)
        t = jnp.where(row[:size, :size] // rank == lane[:size, :size] // rank, t, 0.0)
        x = dot(mix_ref[...], t)
        c = dot(dot(x, c), x, 1, 1)
        w = x if w is None else dot(x, w)
    h3 = dot(dot(w, h), w, 1, 1)
    (t3,) = eliminate(widened(c), [unit])
    t3 = t3[:, :rank]
    basis_map = dot(t3, w)
    eye = unit[:, :rank]
    system = 255.0 * eye + dot(dot(t3, h3), t3, 1, 1)
    rhs = jnp.broadcast_to(jnp.sum(basis_map * q, axis=1, keepdims=True), block)
    found = []

    def visit(j, inverse, extra):
        y, v = extra
        found.append((y[j : j + 1, :] * inverse[:, 0:1]) * v[j : j + 1, :])

    eliminate(jnp.concatenate([system] * (n // rank), 1), [rhs, basis_map], visit)
    weights = found[0]
    for part in found[1:]:
        weights = weights + part
    increment = dot(jnp.broadcast_to(weights, (8, n)), s_ref[...])
    for i in range(8):
        out_ref[i : i + 1, :] = mean_ref[i : i + 1, :] + increment[0:1, i * 128 : (i + 1) * 128]


def analysis(sums, mixers, s, mean):
    return pl.pallas_call(
        analysis_kernel,
        in_specs=[VMEM] * 6,
        out_specs=VMEM,
        out_shape=shape(8, 128),
        compiler_params=params(),
        cost_estimate=cost(16 << 20),
        name="analysis",
    )(sums, *mixers, s, mean)


def add_kernel(a_ref, b_ref, c_ref, d_ref, *rest):
    rest[-1][...] = (a_ref[...] + b_ref[...]) + (c_ref[...] + d_ref[...])


def add_up(a, b, c, d, *tokens):
    return pl.pallas_call(
        add_kernel,
        in_specs=[VMEM] * 4 + [ANY] * len(tokens),
        out_specs=VMEM,
        out_shape=shape(*a.shape),
        compiler_params=params(),
        cost_estimate=cost(1 << 18),
        name="add_up",
    )(a, b, c, d, *tokens)


def to_next(v):
    size = lax.axis_size("tile")
    return lax.ppermute(v, "tile", [(i, i + 1) for i in range(size - 1)])


def to_previous(v):
    size = lax.axis_size("tile")
    return lax.ppermute(v, "tile", [(i + 1, i) for i in range(size - 1)])


def across(v, axis, bits):
    return lax.ppermute(v, axis, [(i, i ^ bits) for i in range(lax.axis_size(axis))])


def local(prior, k, slots, merge, cells, values, var):
    members, levels, rows, width = prior.shape
    rank = merge.shape[2]
    groups = lax.axis_size("grp")
    tile, group = lax.axis_index("tile"), lax.axis_index("grp")
    chip, core = group // 2, group % 2
    place = jnp.stack([tile, group]).astype(jnp.int32)
    sums, low, high = pair_sums(prior, slots, k, rank)
    before = to_next(high)
    after = to_previous(low)

    lo, hi = pack(prior, 0, CHUNKS[0], low)
    arrived_a = to_next(hi), to_previous(lo)
    obs, *mixers = sensors(place, cells, values, var, merge, width // groups, lo)
    pieces = surface(sums, before, after, k, groups, obs)
    pieces = pieces.reshape(groups // 2, 2, rows, rank, width // groups)

    mine = lax.dynamic_index_in_dim(pieces, core, 1, False)
    other = lax.dynamic_index_in_dim(pieces, 1 - core, 1, False)
    pairs = jnp.stack([mine, across(other, "grp", 1)], 1)

    def pair_for(bits):
        return lax.dynamic_index_in_dim(pairs, chip ^ bits, 0, False)

    own = pair_for(0)
    r1, r3, r2 = (across(pair_for(bits), "grp", 2 * bits) for bits in (1, 3, 2))
    lo, hi = pack(prior, 8 * CHUNKS[0], CHUNKS[1], own)
    r1, r2, r3, *arrived_a = lax.optimization_barrier((r1, r2, r3, *arrived_a))
    part, sketches, mean = gram(place, obs, own, r1, r2, r3, lo)
    lo, hi, part = lax.optimization_barrier((lo, hi, part))

    half = part.reshape(2, -1, part.shape[1])
    total = lax.dynamic_index_in_dim(half, core, 0, False) + across(
        lax.dynamic_index_in_dim(half, 1 - core, 0, False), "grp", 1
    )

    def others(v, axis, near):
        return [across(v, axis, near * bits) for bits in (1, 2, 3)]

    arrived_b = to_next(hi), to_previous(lo)
    parts = others(total, "grp", 2)
    lo, hi = pack(prior, 8 * sum(CHUNKS[:2]), CHUNKS[2], part)
    out, done = two_steps(prior, *arrived_a, k, before, after, None, 0, lo)
    lo, hi, done = lax.optimization_barrier((lo, hi, done))
    arrived_c = to_next(hi), to_previous(lo)
    out, done = two_steps(prior, *arrived_b, k, before, after, out, 8 * CHUNKS[0], done)
    total = add_up(total, *parts, done)
    total = add_up(total, *others(total, "tile", 4))
    total, *arrived_c = lax.optimization_barrier((total, *arrived_c))
    parts = others(total, "tile", 1)
    out, done = two_steps(prior, *arrived_c, k, before, after, out, 8 * sum(CHUNKS[:2]), total)
    total = add_up(total, *parts, done)
    second = across(total, "grp", 1)
    both = jnp.where(core == 0, jnp.concatenate([total, second], 0), jnp.concatenate([second, total], 0))
    posterior = analysis(both, mixers, sketches, mean)
    return out, posterior


def solution(mesh):
    in_specs = (P("grp", None, "tile", None), P(None, "tile", None), P("grp"), P(), P(), P(), P())
    out_specs = (P("grp", None, "tile", None), P("tile", "grp"))
    return jax.shard_map(local, mesh=mesh, in_specs=in_specs, out_specs=out_specs, check_vma=False)
```

```python
import functools

import jax
import jax.numpy as jnp
from jax import lax
from jax.experimental import pallas as pl
from jax.experimental.pallas import tpu as pltpu
from jax.sharding import PartitionSpec as P

HI = lax.Precision.HIGHEST
VMEM = pl.BlockSpec(memory_space=pltpu.VMEM)
SMEM = pl.BlockSpec(memory_space=pltpu.SMEM)
ANY = pl.BlockSpec(memory_space=pl.ANY)
HBM = pl.BlockSpec(memory_space=pltpu.HBM)
ROWS = 8
LIMIT = 16 << 20
LARGE = 105 << 19
CHUNKS = (1, 3)
F32 = jnp.float32


def shape(*dims):
    return jax.ShapeDtypeStruct(dims, F32)


def cost(nbytes, flops=0):
    return pl.CostEstimate(flops=flops, bytes_accessed=nbytes, transcendentals=0)


def params(limit=LIMIT):
    return pltpu.CompilerParams(vmem_limit_bytes=limit)


def lanes_sum(v):
    tiles = [v[:, t : t + 128] for t in range(0, v.shape[1], 128)]
    lane = lax.broadcasted_iota(jnp.int32, tiles[0].shape, 1)
    first, last = lane == 0, lane == 127
    ups = [jnp.zeros_like(tiles[0])] + [pltpu.roll(t, 1, 1) for t in tiles]
    downs = [pltpu.roll(t, 127, 1) for t in tiles] + [jnp.zeros_like(tiles[0])]
    out = [
        jnp.where(first, ups[t], ups[t + 1]) + jnp.where(last, downs[t + 1], downs[t])
        for t in range(len(tiles))
    ]
    return jnp.concatenate(out, 1)


def pair_kernel(slot_ref, k_ref, u_ref, sum_ref, low_ref, high_ref, pair_ref, seen_ref, order_ref, sem, k_sem):
    members, levels = u_ref.shape[:2]
    rank = sum_ref.shape[2]
    at = pl.ds(3 * rank, levels)
    turned = [
        pltpu.make_async_copy(k_ref.at[:, 0, :], low_ref.at[at], k_sem.at[0]),
        pltpu.make_async_copy(k_ref.at[:, ROWS - 1, :], high_ref.at[at], k_sem.at[1]),
    ]
    for copy in turned:
        copy.start()
    for s in range(rank):
        seen_ref[s] = 0

    def place(m, carry):
        s = slot_ref[m]
        which = jnp.minimum(seen_ref[s], 1)
        order_ref[2 * s + which] = m
        seen_ref[s] = which + 1
        return carry

    lax.fori_loop(0, members, place, 0)
    copies = [
        pltpu.make_async_copy(
            u_ref.at[order_ref[2 * s + i], pl.ds(levels - 3, 3)], pair_ref.at[i, :, :, s, :], sem.at[i, s]
        )
        for s in range(rank)
        for i in range(2)
    ]
    for copy in copies:
        copy.start()
    for copy in turned + copies:
        copy.wait()
    for l in range(3):
        for x in range(ROWS):
            sum_ref[l, x] = pair_ref[0, l, x] + pair_ref[1, l, x]
    for part, (level, x) in enumerate(((1, 0), (2, 0), (2, 1))):
        at = pl.ds(part * rank, rank)
        low_ref[at, :] = sum_ref[level, x]
        high_ref[at, :] = sum_ref[level, ROWS - 1 - x]


def pair_sums(prior, slots, k, rank):
    members, levels, rows, width = prior.shape
    edge = 3 * rank + levels
    return pl.pallas_call(
        pair_kernel,
        in_specs=[SMEM, HBM, HBM],
        out_specs=[VMEM] * 3,
        out_shape=[
            shape(3, rows, rank, width),
            shape(edge, width),
            shape(edge, width),
        ],
        scratch_shapes=[
            pltpu.VMEM((2, 3, rows, rank, width), F32),
            pltpu.SMEM((rank,), jnp.int32),
            pltpu.SMEM((members,), jnp.int32),
            pltpu.SemaphoreType.DMA((2, rank)),
            pltpu.SemaphoreType.DMA((2,)),
        ],
        compiler_params=params(54 << 20),
        cost_estimate=cost(6 << 20),
        name="pair_sums",
    )(slots, k, prior)


def pack_kernel(first, u_ref, *rest):
    low_ref, high_ref, sem = rest[-3:]
    groups, depth, _, span, _ = low_ref.shape
    copies = []
    for g in range(groups):
        for m in range(span):
            for r in range(depth):
                for side, (ref, x) in enumerate(((low_ref, r), (high_ref, ROWS - 1 - r))):
                    copies.append(
                        pltpu.make_async_copy(
                            u_ref.at[first + g * span + m, :, x, :], ref.at[g, r, :, m, :], sem.at[g, m, r, side]
                        )
                    )
    for copy in copies:
        copy.start()
    for copy in copies:
        copy.wait()


def pack(prior, first, groups, *tokens):
    levels, width = prior.shape[1], prior.shape[3]
    return pl.pallas_call(
        functools.partial(pack_kernel, first),
        in_specs=[HBM] + [ANY] * len(tokens),
        out_specs=[VMEM] * 2,
        out_shape=[shape(groups, 2, levels, 8, width)] * 2,
        scratch_shapes=[pltpu.SemaphoreType.DMA((groups, 8, 2, 2))],
        compiler_params=params(LARGE),
        cost_estimate=cost(groups << 21),
        name="pack_edges",
    )(prior, *tokens)


def step_kernel(first, u_ref, before_ref, after_ref, k_ref, kb_ref, ka_ref, *rest):
    out_ref, token_ref, u, v, w, in_sem, edge_sem, out_sem = rest[-8:]
    token_ref[...] = jnp.zeros_like(token_ref)
    levels, span, width = u_ref.shape[1], u.shape[3], u.shape[4]
    groups = before_ref.shape[0]
    part = levels // 4

    def fetch(g, p):
        slot = g % 2
        at, to = pl.ds(p * part, part), pl.ds(p * part + 1, part)
        copies = [
            pltpu.make_async_copy(
                u_ref.at[first + g * span + m, at], u.at[slot, to, pl.ds(2, ROWS), m, :], in_sem.at[slot, p, m]
            )
            for m in range(span)
        ]
        for r in range(2):
            for side, (ref, x) in enumerate(((before_ref, 1 - r), (after_ref, ROWS + 2 + r))):
                copies.append(
                    pltpu.make_async_copy(ref.at[g, r, at], u.at[slot, to, x], edge_sem.at[slot, p, r, side])
                )
        return copies

    def store(g, p):
        slot, at = g % 2, pl.ds(p * part, part)
        return [
            pltpu.make_async_copy(
                w.at[slot, at, :, m, :], out_ref.at[first + g * span + m, at], out_sem.at[slot, p, m]
            )
            for m in range(span)
        ]

    parts = levels // part
    for p in range(parts):
        for copy in fetch(0, p):
            copy.start()
    zero = jnp.zeros((span, width), F32)
    for l in (0, levels + 1):
        for x in range(ROWS + 4):
            for slot in range(u.shape[0]):
                u[slot, l, x] = zero
        for x in range(ROWS + 2):
            v[l, x] = zero
    tile = (span, 128)
    lane = lax.broadcasted_iota(jnp.int32, tile, 1)
    left, right = lane == 0, lane == 127

    def tiles(ref, l, x):
        return [ref[l, x, :, t : t + 128] for t in range(0, width, 128)]

    def one_step(src, l, x, rows, k):
        blank = jnp.zeros(tile, F32)
        before, here, after = rows
        ups = [blank] + [pltpu.roll(h, 1, 1) for h in here]
        downs = [pltpu.roll(h, 127, 1) for h in here] + [blank]
        out = []
        for t, h in enumerate(here):
            cut = pl.ds(t * 128, 128)
            total = (before[t] + after[t]) + (src[l - 1, x, :, cut] + src[l + 1, x, :, cut])
            total += jnp.where(left, ups[t], ups[t + 1]) + jnp.where(right, downs[t + 1], downs[t])
            out.append(h + k[:, t * 128 : t * 128 + 128] * (total - 6.0 * h))
        return out

    for g in range(groups):
        slot = g % 2
        if g + 1 < groups:
            for p in range(parts):
                for copy in fetch(g + 1, p):
                    copy.start()
        if g >= 2:
            for p in range(parts):
                for copy in store(g - 2, p):
                    copy.wait()

        def first_step(l):
            rows = [tiles(u.at[slot], l + 1, x) for x in range(2)]
            for x in range(-1, ROWS + 1):
                rows = rows[-2:] + [tiles(u.at[slot], l + 1, x + 3)]
                if x < 0:
                    k = kb_ref[l : l + 1, :]
                elif x == ROWS:
                    k = ka_ref[l : l + 1, :]
                else:
                    k = k_ref[l, x : x + 1, :]
                for t, tile_out in enumerate(one_step(u.at[slot], l + 1, x + 2, rows, k)):
                    v[l + 1, x + 1, :, t * 128 : t * 128 + 128] = tile_out

        def second_step(l):
            rows = [tiles(v, l + 1, x) for x in range(2)]
            for x in range(ROWS):
                rows = rows[-2:] + [tiles(v, l + 1, x + 2)]
                for t, tile_out in enumerate(one_step(v, l + 1, x + 1, rows, k_ref[l, x : x + 1, :])):
                    w[slot, l, x, :, t * 128 : t * 128 + 128] = tile_out

        for copy in fetch(g, 0):
            copy.wait()
        first_step(0)
        done = 0
        for p in range(parts):
            if p + 1 < parts:
                for copy in fetch(g, p + 1):
                    copy.wait()
            top = (p + 1) * part if p + 1 < parts else levels - 1
            for l in range(done + 1, top + 1):
                first_step(l)
                second_step(l - 1)
            done = top
            if p + 1 < parts:
                for copy in store(g, p):
                    copy.start()
        second_step(levels - 1)
        for copy in store(g, parts - 1):
            copy.start()
    for g in range(max(groups - 2, 0), groups):
        for p in range(parts):
            for copy in store(g, p):
                copy.wait()


def two_steps(prior, before, after, k, kb, ka, done, first, *tokens):
    members, levels, rows, width = prior.shape
    slots = min(before.shape[0], 2)
    operands = [prior, before, after, k, kb, ka]
    specs = [HBM] + [ANY] * 2 + [VMEM] * 3
    aliases = {}
    if done is not None:
        operands.append(done)
        specs.append(HBM)
        aliases = {6: 0}
    return pl.pallas_call(
        functools.partial(step_kernel, first),
        in_specs=specs + [ANY] * len(tokens),
        out_specs=[HBM, VMEM],
        out_shape=[shape(*prior.shape), shape(8, 128)],
        scratch_shapes=[
            pltpu.VMEM((slots, levels + 2, rows + 4, 8, width), F32),
            pltpu.VMEM((levels + 2, rows + 2, 8, width), F32),
            pltpu.VMEM((slots, levels, rows, 8, width), F32),
            pltpu.SemaphoreType.DMA((slots, 4, 8)),
            pltpu.SemaphoreType.DMA((slots, 4, 2, 2)),
            pltpu.SemaphoreType.DMA((slots, 4, 8)),
        ],
        input_output_aliases=aliases,
        compiler_params=params(LARGE),
        cost_estimate=cost(before.shape[0] << 23),
        name="two_steps",
    )(*operands, *tokens)


def surface_kernel(p_ref, before_ref, after_ref, k_ref, *rest):
    out_ref = rest[-1]
    rank = p_ref.shape[2]
    top = before_ref.shape[0] - 1

    def edge(ref, x):
        low, near, far = (ref[i * rank : (i + 1) * rank, :] for i in range(3))
        k = ref[top : top + 1, :]
        return near + k * (low + far + p_ref[2, x] + lanes_sum(near) - 6.0 * near)

    v6, v7 = [], [edge(before_ref, 0)]
    for x in range(ROWS):
        u6, u7 = p_ref[1, x], p_ref[2, x]

        def beside(level, part):
            before = p_ref[level, x - 1] if x > 0 else before_ref[part * rank : (part + 1) * rank, :]
            after = p_ref[level, x + 1] if x < ROWS - 1 else after_ref[part * rank : (part + 1) * rank, :]
            return before + after

        v6.append(u6 + k_ref[0, x : x + 1, :] * (beside(1, 0) + lanes_sum(u6) + p_ref[0, x] + u7 - 6.0 * u6))
        v7.append(u7 + k_ref[1, x : x + 1, :] * (beside(2, 1) + lanes_sum(u7) + u6 - 6.0 * u7))
    v7.append(edge(after_ref, ROWS - 1))
    piece = out_ref.shape[3]
    for x in range(ROWS):
        here = v7[x + 1]
        total = v7[x] + v7[x + 2] + lanes_sum(here) + v6[x]
        out = here + k_ref[1, x : x + 1, :] * (total - 6.0 * here)
        for g in range(out_ref.shape[0]):
            out_ref[g, x] = out[:, g * piece : (g + 1) * piece]


def surface(sums, before, after, k, groups, *tokens):
    _, rows, rank, width = sums.shape
    levels = k.shape[0]
    edge = pl.BlockSpec(before.shape, lambda i: (0, 0))
    return pl.pallas_call(
        surface_kernel,
        grid=(1,),
        in_specs=[
            pl.BlockSpec(sums.shape, lambda i: (0, 0, 0, 0)),
            edge,
            edge,
            pl.BlockSpec((2, rows, width), lambda i: (levels // 2 - 1, 0, 0)),
        ]
        + [ANY] * len(tokens),
        out_specs=pl.BlockSpec((groups, rows, rank, width // groups), lambda i: (0, 0, 0, 0)),
        out_shape=shape(groups, rows, rank, width // groups),
        compiler_params=params(),
        cost_estimate=cost(4 << 20),
        name="surface_steps",
    )(sums, before, after, k, *tokens)


def sensor_kernel(at_ref, cell_ref, value_ref, var_ref, m_ref, *rest):
    rank = m_ref.shape[2]
    out_ref, *mix_refs = rest[-1 - m_ref.shape[0] :]
    for level, ref in enumerate(mix_refs):
        ref[...] = jnp.zeros_like(ref)
        turned = m_ref[level].T
        for p in range(ref.shape[0] // rank):
            ref[p * rank : (p + 1) * rank, 2 * p * rank : 2 * (p + 1) * rank] = turned
    width, columns = 1024, out_ref.shape[1]
    rows = out_ref.shape[0] // 2
    chunks, span = cell_ref.shape
    weight = 1.0 / var_ref[...]
    local = cell_ref[...] - at_ref[0] * (rows * width)
    x = local // width
    y = local - x * width - at_ref[1] * columns
    left, right = [], []
    row = lax.broadcasted_iota(jnp.int32, (rows, span), 0)
    column = lax.broadcasted_iota(jnp.int32, (columns, span), 0)
    weighted = weight * value_ref[...]
    for c in range(chunks):
        hit = x[c : c + 1, :] == row
        left.append(
            jnp.concatenate(
                [jnp.where(hit, weight[c : c + 1, :], 0.0), jnp.where(hit, weighted[c : c + 1, :], 0.0)], 0
            )
        )
        right.append(jnp.where(y[c : c + 1, :] == column, 1.0, 0.0))
    out_ref[...] = lax.dot_general(
        jnp.concatenate(left, 1),
        jnp.concatenate(right, 1),
        (((1,), (1,)), ((), ())),
        precision=HI,
        preferred_element_type=F32,
    )


def sensors(place, cells, values, var, merge, columns, *tokens):
    rank = merge.shape[2]
    mixers = [shape(rank << i, 2 * rank << i) for i in range(merge.shape[0])][::-1]
    return pl.pallas_call(
        sensor_kernel,
        in_specs=[SMEM] + [VMEM] * 4 + [ANY] * len(tokens),
        out_specs=[VMEM] * (1 + len(mixers)),
        out_shape=[shape(16, columns)] + mixers,
        compiler_params=params(),
        cost_estimate=cost(4 << 20),
        name="sensor_sums",
    )(place, *(a.reshape(-1, 128) for a in (cells, values, var)), merge, *tokens)


def gram_kernel(place_ref, obs_ref, own_ref, r1_ref, r2_ref, r3_ref, *rest):
    sums_ref, s_ref, mean_ref, raw_ref = rest[-4:]
    chip, core = place_ref[1] // 2, place_ref[1] % 2
    for d, ref in ((0, own_ref), (1, r1_ref), (2, r2_ref), (3, r3_ref)):
        for slot in range(2):
            group = jnp.bitwise_xor(chip, d) * 2 + jnp.bitwise_xor(core, slot)
            rank = ref.shape[2]
            at = pl.ds(pl.multiple_of(group * rank, rank), rank)
            for x in range(ROWS):
                raw_ref[x, at, :] = ref[slot, x]
    total = None
    sketches = raw_ref.shape[1]
    member_total = 2 * sketches
    for x in range(0, 8, 2):
        both, means, weights, values = [], [], [], []
        for i in (x, x + 1):
            raw = raw_ref[i]
            mean = jnp.sum(raw, axis=0, keepdims=True) * (1.0 / member_total)
            dev = raw - 2.0 * mean
            s_ref[:, i * 128 : (i + 1) * 128] = dev
            mean_ref[i : i + 1, :] = mean
            both.append(dev)
            w = obs_ref[i : i + 1, :]
            weights.append(w)
            values.append(obs_ref[8 + i : 9 + i, :] - mean * w)
        dev = jnp.concatenate(both, 1)
        w = jnp.concatenate(weights, 1)
        z = jnp.broadcast_to(jnp.concatenate(values, 1), (8, dev.shape[1]))
        left = jnp.concatenate([dev, dev * w, z], 0)
        part = lax.dot_general(left, dev, (((1,), (1,)), ((), ())), precision=HI, preferred_element_type=F32)
        total = part if total is None else total + part
    gram, weighted, rhs = total[:sketches], total[sketches : 2 * sketches], total[2 * sketches :]
    row = lax.broadcasted_iota(jnp.int32, gram.shape, 0)
    lane = lax.broadcasted_iota(jnp.int32, gram.shape, 1)
    sums_ref[0:sketches, :] = jnp.where(lane > row, gram, weighted)
    sums_ref[sketches : sketches + 8, :] = jnp.broadcast_to(
        jnp.sum(jnp.where(lane == row, gram, 0.0), axis=0, keepdims=True), (8, 128)
    )
    sums_ref[sketches + 8 : sketches + 16, :] = rhs


def gram(place, obs, own, r1, r2, r3, *tokens):
    return pl.pallas_call(
        gram_kernel,
        in_specs=[SMEM] + [VMEM] * 5 + [ANY] * len(tokens),
        out_specs=[VMEM] * 3,
        out_shape=[shape(144, 128), shape(128, 1024), shape(8, 128)],
        scratch_shapes=[pltpu.VMEM((8, 128, 128), F32)],
        compiler_params=params(),
        cost_estimate=cost(4 << 20),
        name="gram_sums",
    )(place, obs, own, r1, r2, r3, *tokens)


def dot(a, b, ca=1, cb=0):
    return lax.dot_general(a, b, (((ca,), (cb,)), ((), ())), precision=HI, preferred_element_type=F32)


def analysis_kernel(sums_ref, mix0_ref, mix1_ref, mix2_ref, s_ref, mean_ref, out_ref):
    n = 128
    mixers = (mix0_ref, mix1_ref, mix2_ref)
    rank = mix2_ref.shape[0]
    packed = sums_ref[0:n, :]
    row = lax.broadcasted_iota(jnp.int32, (n, n), 0)
    lane = lax.broadcasted_iota(jnp.int32, (n, n), 1)
    upper = jnp.where(lane > row, packed, 0.0)
    lower = jnp.where(lane < row, packed, 0.0)
    g = upper + upper.T + jnp.where(lane == row, sums_ref[n : n + 1, :], 0.0)
    h = lower + lower.T + jnp.where(lane == row, packed, 0.0)
    q = sums_ref[n + 8 : n + 9, :]

    block = (rank, n)
    sub = lax.broadcasted_iota(jnp.int32, block, 0)
    at = lax.broadcasted_iota(jnp.int32, block, 1)
    unit = jnp.where(at % rank == sub, 1.0, 0.0)

    def eliminate(d, extra, visit=None):
        columns = [jnp.take_along_axis(d, at // rank * rank + j, axis=1) for j in range(rank)]
        for j in range(rank):
            c = columns[j]
            inverse = 1.0 / c[j : j + 1, :]
            if visit is not None:
                visit(j, inverse, extra)
            if j == rank - 1:
                break
            factor = jnp.where(sub > j, c * inverse, 0.0)
            for k in range(j + 1, rank):
                columns[k] = columns[k] - factor * c[k : k + 1, :]
            extra = [e - factor * e[j : j + 1, :] for e in extra]
        return extra

    def widened(v):
        if v.shape[1] == n:
            return v
        return jnp.concatenate([v, jnp.zeros((rank, n - v.shape[1]), F32)], 1) + jnp.where(
            at >= v.shape[1], unit, 0.0
        )

    c = g
    w = None
    for mix_ref in mixers:
        size = c.shape[0]
        d = jnp.zeros((rank, size), F32)
        for b in range(size // rank):
            d = d + jnp.where(at[:, :size] // rank == b, c[b * rank : (b + 1) * rank, :], 0.0)
        (t,) = eliminate(widened(d), [unit])
        t = jnp.concatenate([t[:, :size]] * (size // rank), 0)
        t = jnp.where(row[:size, :size] // rank == lane[:size, :size] // rank, t, 0.0)
        x = dot(mix_ref[...], t)
        c = dot(dot(x, c), x, 1, 1)
        w = x if w is None else dot(x, w)
    h3 = dot(dot(w, h), w, 1, 1)
    (t3,) = eliminate(widened(c), [unit])
    t3 = t3[:, :rank]
    basis_map = dot(t3, w)
    eye = unit[:, :rank]
    system = 255.0 * eye + dot(dot(t3, h3), t3, 1, 1)
    rhs = jnp.broadcast_to(jnp.sum(basis_map * q, axis=1, keepdims=True), block)
    found = []

    def visit(j, inverse, extra):
        y, v = extra
        found.append((y[j : j + 1, :] * inverse[:, 0:1]) * v[j : j + 1, :])

    eliminate(jnp.concatenate([system] * (n // rank), 1), [rhs, basis_map], visit)
    weights = found[0]
    for part in found[1:]:
        weights = weights + part
    increment = dot(jnp.broadcast_to(weights, (8, n)), s_ref[...])
    for i in range(8):
        out_ref[i : i + 1, :] = mean_ref[i : i + 1, :] + increment[0:1, i * 128 : (i + 1) * 128]


def analysis(sums, mixers, s, mean):
    return pl.pallas_call(
        analysis_kernel,
        in_specs=[VMEM] * 6,
        out_specs=VMEM,
        out_shape=shape(8, 128),
        compiler_params=params(),
        cost_estimate=cost(16 << 20),
        name="analysis",
    )(sums, *mixers, s, mean)


def add_kernel(a_ref, b_ref, c_ref, d_ref, *rest):
    rest[-1][...] = (a_ref[...] + b_ref[...]) + (c_ref[...] + d_ref[...])


def add_up(a, b, c, d, *tokens):
    return pl.pallas_call(
        add_kernel,
        in_specs=[VMEM] * 4 + [ANY] * len(tokens),
        out_specs=VMEM,
        out_shape=shape(*a.shape),
        compiler_params=params(),
        cost_estimate=cost(1 << 18),
        name="add_up",
    )(a, b, c, d, *tokens)


def to_next(v):
    size = lax.axis_size("tile")
    return lax.ppermute(v, "tile", [(i, i + 1) for i in range(size - 1)])


def to_previous(v):
    size = lax.axis_size("tile")
    return lax.ppermute(v, "tile", [(i + 1, i) for i in range(size - 1)])


def across(v, axis, bits):
    return lax.ppermute(v, axis, [(i, i ^ bits) for i in range(lax.axis_size(axis))])


def local(prior, k, slots, merge, cells, values, var):
    members, levels, rows, width = prior.shape
    rank = merge.shape[2]
    groups = lax.axis_size("grp")
    tile, group = lax.axis_index("tile"), lax.axis_index("grp")
    chip, core = group // 2, group % 2
    place = jnp.stack([tile, group]).astype(jnp.int32)
    sums, low, high = pair_sums(prior, slots, k, rank)
    before = to_next(high)
    after = to_previous(low)
    kb, ka = before[3 * rank :], after[3 * rank :]

    lo, hi = pack(prior, 0, CHUNKS[0], low)
    arrived_a = to_next(hi), to_previous(lo)
    obs, *mixers = sensors(place, cells, values, var, merge, width // groups, lo)
    pieces = surface(sums, before, after, k, groups, obs)
    pieces = pieces.reshape(groups // 2, 2, rows, rank, width // groups)

    mine = lax.dynamic_index_in_dim(pieces, core, 1, False)
    other = lax.dynamic_index_in_dim(pieces, 1 - core, 1, False)
    pairs = jnp.stack([mine, across(other, "grp", 1)], 1)

    def pair_for(bits):
        return lax.dynamic_index_in_dim(pairs, chip ^ bits, 0, False)

    own = pair_for(0)
    r1, r3, r2 = (across(pair_for(bits), "grp", 2 * bits) for bits in (1, 3, 2))
    lo, hi = pack(prior, 8 * CHUNKS[0], CHUNKS[1], r1)
    r1, r2, r3, *arrived_a = lax.optimization_barrier((r1, r2, r3, *arrived_a))
    part, sketches, mean = gram(place, obs, own, r1, r2, r3, lo)

    half = part.reshape(2, -1, part.shape[1])
    total = lax.dynamic_index_in_dim(half, core, 0, False) + across(
        lax.dynamic_index_in_dim(half, 1 - core, 0, False), "grp", 1
    )

    def others(v, axis, near):
        return [across(v, axis, near * bits) for bits in (1, 2, 3)]

    arrived_b = to_next(hi), to_previous(lo)
    parts = others(total, "grp", 2)
    out, done = two_steps(prior, *arrived_a, k, kb, ka, None, 0, part)
    total = add_up(total, *parts, done)
    total = add_up(total, *others(total, "tile", 4), *arrived_b)
    parts = others(total, "tile", 1)
    out, done = two_steps(prior, *arrived_b, k, kb, ka, out, 8 * CHUNKS[0], total)
    total = add_up(total, *parts, done)
    second = across(total, "grp", 1)
    both = jnp.where(core == 0, jnp.concatenate([total, second], 0), jnp.concatenate([second, total], 0))
    posterior = analysis(both, mixers, sketches, mean)
    return out, posterior


def solution(mesh):
    in_specs = (P("grp", None, "tile", None), P(None, "tile", None), P("grp"), P(), P(), P(), P())
    out_specs = (P("grp", None, "tile", None), P("tile", "grp"))
    return jax.shard_map(local, mesh=mesh, in_specs=in_specs, out_specs=out_specs, check_vma=False)
```
